32 devices in a mesh: lon: 4 (over x, core), lat: 8 (over z, y).
Axes of the slice: x: 2, y: 2, z: 4, core: 2. Of those that a mesh axis runs over, the one named last changes fastest.
Arguments:
- ocean_status: float32 [128, 3, 64, 2048], P(None, None, 'lat', 'lon'), may hold values from -4 to 4
- height_driver: bfloat16 [128, 64, 2048], P(None, 'lat', 'lon'), may hold values from -4 to 4
- obs_index: int32 [8, 4, 64], P('lat', 'lon'), may hold values from 0 to 4095
- obs_value: float32 [8, 4, 64], P('lat', 'lon'), may hold values from -5 to 5
- obs_error: float32 [8, 4, 64], P('lat', 'lon'), may hold values from 1 to 10
Outputs:
- analysis: float32 [128, 3, 64, 2048], P(None, None, 'lat', 'lon')
The draws below stay inside these ranges and needn't reach their ends.
Inputs may be any that keep to these rules, and one draw needn't show every extreme that they name: `obs_index`: an observation's cell inside its device's tile, the tile's row times 512 plus its column.
All inputs are finite; a program needn't handle non-finite values.
Results may differ from the reference program's by a relative error of at most 0.0003.
Values sent between devices are 32-bit elements; how exact they have to be, the bound alone decides.
A program may use at most 128 MiB of HBM per device.

```python
import math
import jax
import jax.numpy as jnp
from jax import lax

MEMBERS = 128
CLAT = 8
CLON = 512
OBS_DEV = 64
NS_ITERS = 14
NLAT = 64
NLON = 2048
N_LON = 4
N_LAT = 8


def touch_ends(array, stream_key, least, high):
    longest = array.shape.index(max(array.shape))
    spots = []
    for shift in (0, 1):
        where = [jax.random.randint(jax.random.fold_in(stream_key, axis), (), 0, length) for axis, length in enumerate(array.shape)]
        where[longest] = (where[longest] + shift) % array.shape[longest]
        spots.append(tuple(where))
    return array.at[spots[0]].set(least).at[spots[1]].set(high)


def shard_levels(rng, extent, pieces, least, largest):
    level = 1.0
    for position, parts in pieces:
        steps = jax.random.uniform(jax.random.fold_in(jax.random.fold_in(rng, 6), position), (parts,), jnp.float32, least / len(pieces), largest / len(pieces))
        level = level * jnp.repeat(jnp.exp(steps), extent[position] // parts).reshape((-1,) + (1,) * (len(extent) - 1 - position))
    return level


def noise(rng, dims, scale, most, split=(), kind=jnp.bfloat16):
    loudness = shard_levels(rng, dims, split, -0.22, 0.18) if split else 1.0
    entries = jax.random.normal(rng, dims, jnp.float32) * scale * loudness
    return jnp.minimum(jnp.maximum(entries, -most), most).astype(kind)


def setup_inputs(seed: int = 0) -> dict:
    key_list = jax.random.split(jax.random.key(seed), 6)
    ocean_status = noise(key_list[0], (MEMBERS, 3, NLAT, NLON), 1.0, 4.0, ((2, 8), (3, 4)), jnp.float32)
    height_driver = noise(key_list[1], (MEMBERS, NLAT, NLON), 1.0, 4.0, ((1, 8), (2, 4)))
    obs_index = touch_ends(jax.random.randint(key_list[2], (N_LAT, N_LON, OBS_DEV), 0, CLAT * CLON), jax.random.fold_in(key_list[2], 1), 0, (CLAT * CLON) - 1).astype(jnp.int32)
    obs_value = noise(key_list[3], (N_LAT, N_LON, OBS_DEV), 1.0, 5.0, ((0, 8), (1, 4)), jnp.float32)
    obs_error = jnp.clip(jnp.exp(math.log(10.0) - 2.3025851 * jax.random.uniform(key_list[4], (N_LAT, N_LON, OBS_DEV), jnp.float32) ** shard_levels(key_list[4], (N_LAT, N_LON, OBS_DEV), ((0, 8), (1, 4)), -0.2, 0.2)), 1.0, 10.0)
    return {"ocean_status": ocean_status, "height_driver": height_driver, "obs_index": obs_index, "obs_value": obs_value, "obs_error": obs_error}


PRECISE = lax.Precision.HIGHEST
GRAVITY = 1.0
DEPTH_MEAN = 1.0
COURANT = 0.2
DIFFUSION = 0.1
FORCE_STEP = 0.5
CORIOLIS_MAX = 0.3

def centre(field):
    return field[..., 1:-1, 1:-1]

def east_of(field):
    return field[..., 1:-1, 2:]

def west_of(field):
    return field[..., 1:-1, :-2]

def north_of(field):
    return field[..., 2:, 1:-1]

def south_of(field):
    return field[..., :-2, 1:-1]

def along_x(field):
    return 0.5 * (east_of(field) - west_of(field))

def along_y(field):
    return 0.5 * (north_of(field) - south_of(field))

def laplace(field):
    return east_of(field) + west_of(field) + north_of(field) + south_of(field) - 4.0 * centre(field)

def advance(padded, pushes, coriolis):
    height = padded[..., 0, :, :]
    zonal = padded[..., 1, :, :]
    merid = padded[..., 2, :, :]
    height_c = centre(height)
    zonal_c = centre(zonal)
    merid_c = centre(merid)
    flux_x = (DEPTH_MEAN + height) * zonal
    flux_y = (DEPTH_MEAN + height) * merid
    height_new = height_c - COURANT * (along_x(flux_x) + along_y(flux_y)) + DIFFUSION * laplace(height) + FORCE_STEP * pushes
    zonal_new = zonal_c - COURANT * (GRAVITY * along_x(height) + zonal_c * along_x(zonal) + merid_c * along_y(zonal)) + COURANT * coriolis * merid_c + DIFFUSION * laplace(zonal)
    merid_new = merid_c - COURANT * (GRAVITY * along_y(height) + zonal_c * along_x(merid) + merid_c * along_y(merid)) - COURANT * coriolis * zonal_c + DIFFUSION * laplace(merid)
    return jnp.stack([height_new, zonal_new, merid_new], axis=-3)

def pad_grid(fields):
    rows = jnp.pad(fields, [(0, 0)] * (fields.ndim - 2) + [(1, 1), (0, 0)])
    return jnp.concatenate([rows[..., -1:], rows, rows[..., :1]], axis=-1)

def coriolis_rows(start, count, total):
    rows = start + jnp.arange(count, dtype=jnp.float32)
    return (CORIOLIS_MAX * (2.0 * (rows + 0.5) / total - 1.0))[:, None]

def ensemble_weights(gram, innovation_sum, members):
    identity = jnp.eye(members, dtype=jnp.float32)
    amat = (members - 1) * identity + gram
    scale = jnp.sqrt(jnp.sum(amat * amat))
    upper = amat / scale
    lower = identity
    for repeat in range(NS_ITERS):
        factor = 1.5 * identity - 0.5 * jnp.dot(lower, upper, precision=PRECISE)
        upper = jnp.dot(upper, factor, precision=PRECISE)
        lower = jnp.dot(factor, lower, precision=PRECISE)
    root = lower / jnp.sqrt(scale)
    inverse = jnp.dot(root, root, precision=PRECISE)
    mean_shift = jnp.dot(inverse, innovation_sum, precision=PRECISE)
    return math.sqrt(members - 1) * root + mean_shift[:, None]

def observe_sums(measurement_readings, values, errors):
    obs_mean = lax.optimization_barrier(jnp.mean(measurement_readings, axis=0))
    obs_spread = measurement_readings - obs_mean
    innovation = values - obs_mean
    inv_error = 1.0 / errors
    gram = jnp.dot(obs_spread * inv_error, obs_spread.T, precision=PRECISE)
    innovation_sum = jnp.dot(obs_spread, inv_error * innovation, precision=PRECISE)
    return (gram, innovation_sum)

def ensemble_mapping_operator(ensemble, blending_coefficients):
    ens_mean = lax.optimization_barrier(jnp.mean(ensemble, axis=0, keepdims=True))
    spread = ensemble - ens_mean
    return ens_mean + jnp.einsum('kfyx,km->mfyx', spread, blending_coefficients, precision=PRECISE)

def reference(ocean_status, height_driver, obs_index, obs_value, obs_error):
    coriolis = coriolis_rows(0.0, NLAT, NLAT)

    def single_run_projection(member_pair):
        fields, pushes = member_pair
        pushes = pushes.astype(jnp.float32)
        for repeat in range(2):
            fields = advance(pad_grid(fields), pushes, coriolis)
        return fields
    projected_ensemble_states = lax.map(single_run_projection, (ocean_status, height_driver))
    block_north_extent = jnp.arange(N_LAT, dtype=jnp.int32)[:, None, None] * CLAT + obs_index // CLON
    block_east_extent = jnp.arange(N_LON, dtype=jnp.int32)[None, :, None] * CLON + obs_index % CLON
    measurement_readings = projected_ensemble_states[:, 0, block_north_extent.reshape(-1), block_east_extent.reshape(-1)]
    gram, innovation_sum = observe_sums(measurement_readings, obs_value.reshape(-1), obs_error.reshape(-1))
    blending_coefficients = ensemble_weights(gram, innovation_sum, MEMBERS)
    return ensemble_mapping_operator(projected_ensemble_states, blending_coefficients)
```

```python
import functools
import math

import jax
import jax.numpy as jnp
from jax import lax
from jax.experimental import pallas as pl
from jax.experimental.pallas import tpu as pltpu
from jax.sharding import PartitionSpec as P

NS_ITERS = 14
COURANT = 0.2
DIFFUSION = 0.1
FORCE_STEP = 0.5
CORIOLIS_MAX = 0.3
CHUNK = 16
LANES = 128
MESH = pl.DeviceIdType.MESH


def doublings(count):
    return [1 << b for b in range(count.bit_length() - 1)]


def parts_of(x, count):
    parts = []
    for _ in range(count):
        parts.append(x.astype(jnp.bfloat16))
        x = x - parts[-1].astype(jnp.float32)
    return parts


def product(a, b):
    rows, columns = a.shape[0], b.shape[1]
    whole = jnp.dot(jnp.concatenate(parts_of(a, 2), axis=0), jnp.concatenate(parts_of(b, 2), axis=1),
                    preferred_element_type=jnp.float32)
    return (whole[:rows, :columns] + whole[:rows, columns:]) + (whole[rows:, :columns] + whole[rows:, columns:])


def forecast_kernel(n_lat, n_lon, state_hbm, force_ref, index_ref, value_ref, error_ref, fore_hbm, sums_ref,
                    raw, ext, cols_out, cols_in, fore, onehot, readings, acc, acc_in,
                    in_sem, out_sem, row_send, row_recv, col_send, col_recv, sum_send, sum_recv):
    chunks = raw.shape[0]
    members = chunks * CHUNK
    rows, width = raw.shape[3], raw.shape[4]
    lat, lon = lax.axis_index("lat"), lax.axis_index("lon")
    east = (lat, lax.rem(lon + 1, n_lon))
    west = (lat, lax.rem(lon + n_lon - 1, n_lon))
    has_south, has_north = lat > 0, lat < n_lat - 1
    south, north = (jnp.maximum(lat - 1, 0), lon), (jnp.minimum(lat + 1, n_lat - 1), lon)

    def dev(place):
        return {"lat": place[0], "lon": place[1]}

    partners = [(lat, lon ^ d) for d in doublings(n_lon)] + [(lat ^ d, lon) for d in doublings(n_lat)]
    far = [(lat, lon ^ d) for d in doublings(n_lon)[1:]] + [(lat ^ d, lon) for d in doublings(n_lat)[1:]]

    def load(c):
        return pltpu.make_async_copy(state_hbm.at[pl.ds(c * CHUNK, CHUNK)], raw.at[c], in_sem.at[c])

    @pl.loop(0, chunks)
    def _(c):
        load(c).start()

    barrier = pltpu.get_barrier_semaphore()
    for place in [east, west] + far:
        pl.semaphore_signal(barrier, inc=1, device_id=dev(place), device_id_type=MESH)

    @pl.when(has_south)
    def _():
        pl.semaphore_signal(barrier, inc=1, device_id=dev(south), device_id_type=MESH)

    @pl.when(has_north)
    def _():
        pl.semaphore_signal(barrier, inc=1, device_id=dev(north), device_id_type=MESH)

    pl.semaphore_wait(barrier, 2 + len(far) + has_south.astype(jnp.int32) + has_north.astype(jnp.int32))

    def row_copy(step, c, side):
        return pltpu.make_async_remote_copy(
            src_ref=ext.at[step, c, :, rows if side == 0 else 1],
            dst_ref=ext.at[step, c, :, 0 if side == 0 else rows + 1],
            send_sem=row_send.at[step, side, c], recv_sem=row_recv.at[step, side, c],
            device_id=dev(north if side == 0 else south), device_id_type=MESH)

    def col_copy(step, c, side):
        return pltpu.make_async_remote_copy(
            src_ref=cols_out.at[step, side, c], dst_ref=cols_in.at[step, side, c],
            send_sem=col_send.at[step, side, c], recv_sem=col_recv.at[step, side, c],
            device_id=dev(east if side == 0 else west), device_id_type=MESH)

    lane = lax.broadcasted_iota(jnp.int32, (CHUNK, LANES), 1)
    wide = lax.broadcasted_iota(jnp.int32, (CHUNK, width), 1)

    def send(step, c):
        @pl.when(has_north)
        def _():
            row_copy(step, c, 0).start()

        @pl.when(has_south)
        def _():
            row_copy(step, c, 1).start()

        last = jnp.zeros((CHUNK, LANES), jnp.float32)
        first = last
        for f in range(3):
            for r in range(rows):
                j = f * rows + r
                last = jnp.where(lane == j, ext[step, c, f, r + 1, :, width - 1:width], last)
                first = jnp.where(lane == j, ext[step, c, f, r + 1, :, 0:1], first)
        cols_out[step, 0, c] = last
        cols_out[step, 1, c] = first
        col_copy(step, c, 0).start()
        col_copy(step, c, 1).start()

    def receive(step, c):
        @pl.when(has_south)
        def _():
            row_copy(step, c, 0).wait_recv()

        @pl.when(has_north)
        def _():
            row_copy(step, c, 1).wait_recv()

        col_copy(step, c, 0).wait_recv()
        col_copy(step, c, 1).wait_recv()

    @pl.when(lat == 0)
    def _():
        for step in range(2):
            @pl.loop(0, chunks)
            def _(c):
                ext[step, c, :, 0] = jnp.zeros((3, CHUNK, width), jnp.float32)

    @pl.when(lat == n_lat - 1)
    def _():
        for step in range(2):
            @pl.loop(0, chunks)
            def _(c):
                ext[step, c, :, rows + 1] = jnp.zeros((3, CHUNK, width), jnp.float32)

    @pl.loop(0, chunks)
    def _(c):
        load(c).wait()
        for f in range(3):
            ext[0, c, f, pl.ds(1, rows)] = jnp.swapaxes(raw[c, :, f], 0, 1)
        send(0, c)

    total_rows = float(n_lat * rows)
    first_row = (lat * rows).astype(jnp.float32)

    def advance(step, c, put):
        pushes = jnp.swapaxes(force_ref[pl.ds(c * CHUNK, CHUNK)].astype(jnp.float32), 0, 1)
        from_west = cols_in[step, 0, c]
        from_east = cols_in[step, 1, c]
        for r in range(rows):
            coriolis = CORIOLIS_MAX * (2.0 * (first_row + (r + 0.5)) / total_rows - 1.0)

            def around(f):
                mid = ext[step, c, f, r + 1]
                j = f * rows + r
                e = jnp.where(wide == width - 1, from_east[:, j:j + 1], pltpu.roll(mid, width - 1, 1))
                w = jnp.where(wide == 0, from_west[:, j:j + 1], pltpu.roll(mid, 1, 1))
                return mid, e, w, ext[step, c, f, r + 2], ext[step, c, f, r]

            h, he, hw, hn, hs = around(0)
            u, ue, uw, un, us = around(1)
            v, ve, vw, vn, vs = around(2)
            half = 0.5 * COURANT
            h_new = (h - half * (((1.0 + he) * ue - (1.0 + hw) * uw) + ((1.0 + hn) * vn - (1.0 + hs) * vs))
                     + DIFFUSION * (he + hw + hn + hs - 4.0 * h) + FORCE_STEP * pushes[r])
            u_new = (u - half * ((he - hw) + u * (ue - uw) + v * (un - us))
                     + COURANT * coriolis * v + DIFFUSION * (ue + uw + un + us - 4.0 * u))
            v_new = (v - half * ((hn - hs) + u * (ve - vw) + v * (vn - vs))
                     - COURANT * coriolis * u + DIFFUSION * (ve + vw + vn + vs - 4.0 * v))
            put(r, h_new, u_new, v_new)

    @pl.loop(0, chunks)
    def _(c):
        receive(0, c)

        def put(r, *new):
            for f in range(3):
                ext[1, c, f, r + 1] = new[f]

        advance(0, c, put)
        send(1, c)

    for r in range(rows):
        cell = lax.broadcasted_iota(jnp.int32, (width, LANES), 0) + r * width
        onehot[r] = jnp.where(cell == index_ref[0:1, :], 1.0, 0.0).astype(jnp.bfloat16)

    def save(c):
        return pltpu.make_async_copy(fore.at[c], fore_hbm.at[c], out_sem.at[c])

    @pl.loop(0, chunks)
    def _(c):
        receive(1, c)

        def put(r, *new):
            for f in range(3):
                fore[c, f, r] = new[f]

        advance(1, c, put)
        save(c).start()
        seen = jnp.zeros((CHUNK, LANES), jnp.float32)
        for r in range(rows):
            picked = jnp.dot(jnp.concatenate(parts_of(fore[c, 0, r], 3), axis=0), onehot[r],
                             preferred_element_type=jnp.float32)
            seen += (picked[:CHUNK] + picked[CHUNK:2 * CHUNK]) + picked[2 * CHUNK:]
        readings[c] = seen

    seen = readings[...].reshape(members, LANES)
    mean = jnp.mean(seen, axis=0, keepdims=True)
    spread = seen - mean
    inv = 1.0 / error_ref[0:1, :]
    innovation = inv * (value_ref[0:1, :] - mean)
    left = jnp.concatenate([spread * inv, jnp.broadcast_to(innovation, (8, LANES))], axis=0)
    acc[0] = product(left, spread.T)
    swaps = [pltpu.make_async_remote_copy(
        src_ref=acc.at[s], dst_ref=acc_in.at[s], send_sem=sum_send.at[s], recv_sem=sum_recv.at[s],
        device_id=dev(place), device_id_type=MESH) for s, place in enumerate(partners)]
    for s, swap in enumerate(swaps):
        swap.start()
        swap.wait_recv()
        acc[s + 1] = acc[s] + acc_in[s]
    sums_ref[...] = acc[len(swaps)]
    for swap in swaps:
        swap.wait_send()

    @pl.loop(0, chunks)
    def _(c):
        save(c).wait()
        for step in range(2):
            @pl.when(has_north)
            def _():
                row_copy(step, c, 0).wait_send()

            @pl.when(has_south)
            def _():
                row_copy(step, c, 1).wait_send()

            col_copy(step, c, 0).wait_send()
            col_copy(step, c, 1).wait_send()


def analysis_kernel(sums_ref, fore_ref, out_ref, mix):
    members = sums_ref.shape[1]
    rows = fore_ref.shape[2]
    width = fore_ref.shape[4]

    @pl.when(pl.program_id(0) == 0)
    def _():
        eye = (lax.broadcasted_iota(jnp.int32, (members, members), 0)
               == lax.broadcasted_iota(jnp.int32, (members, members), 1)).astype(jnp.float32)
        amat = (members - 1) * eye + sums_ref[:members]
        scale = jnp.sqrt(jnp.sum(jnp.sum(amat * amat, axis=1, keepdims=True), axis=0, keepdims=True))

        def turn(_, pair):
            upper, lower = pair
            factor = 1.5 * eye - 0.5 * product(lower, upper)
            return product(upper, factor), product(factor, lower)

        _, lower = lax.fori_loop(0, NS_ITERS, turn, (amat / scale, eye))
        root = lower / jnp.sqrt(scale)
        inverse = product(root, root)
        shift = product(sums_ref[members:], inverse.T)
        weights = math.sqrt(members - 1) * root.T + shift[0:1, :]
        high = weights.astype(jnp.bfloat16)
        low = (weights - high.astype(jnp.float32)).astype(jnp.bfloat16)
        mix[:members, :members] = high
        mix[:members, members:] = high
        mix[members:, :members] = low
        mix[members:, members:] = jnp.zeros_like(low)

    for r in range(rows):
        cells = fore_ref[:, 0, r].reshape(members, width)
        mean = jnp.mean(cells, axis=0, keepdims=True)
        spread = cells - mean
        high = spread.astype(jnp.bfloat16)
        low = (spread - high.astype(jnp.float32)).astype(jnp.bfloat16)
        both = jnp.dot(mix[...], jnp.concatenate([high, low], axis=0), preferred_element_type=jnp.float32)
        out_ref[:, 0, r, :] = mean + both[:members] + both[members:]


def shards(n_lat, n_lon, ocean_status, height_driver, obs_index, obs_value, obs_error):
    members, fields, rows, width = ocean_status.shape
    chunks = members // CHUNK
    spare = LANES - obs_index.shape[-1]

    def flat(array, fill):
        return jnp.pad(array.reshape(1, -1), ((0, 0), (0, spare)), constant_values=fill)

    vmem = pl.BlockSpec(memory_space=pltpu.VMEM)
    anywhere = pl.BlockSpec(memory_space=pl.ANY)
    stages = len(doublings(n_lon)) + len(doublings(n_lat))
    dma = pltpu.SemaphoreType.DMA
    f32 = jnp.float32
    block = (chunks, fields, rows, CHUNK, width)
    fore, sums = pl.pallas_call(
        functools.partial(forecast_kernel, n_lat, n_lon),
        out_shape=(jax.ShapeDtypeStruct(block, f32), jax.ShapeDtypeStruct((members + 8, members), f32)),
        in_specs=[anywhere, vmem, vmem, vmem, vmem],
        out_specs=(anywhere, vmem),
        scratch_shapes=[
            pltpu.VMEM((chunks, CHUNK, fields, rows, width), f32),
            pltpu.VMEM((2, chunks, fields, rows + 2, CHUNK, width), f32),
            pltpu.VMEM((2, 2, chunks, CHUNK, LANES), f32),
            pltpu.VMEM((2, 2, chunks, CHUNK, LANES), f32),
            pltpu.VMEM(block, f32),
            pltpu.VMEM((rows, width, LANES), jnp.bfloat16),
            pltpu.VMEM((chunks, CHUNK, LANES), f32),
            pltpu.VMEM((stages + 1, members + 8, members), f32),
            pltpu.VMEM((stages, members + 8, members), f32),
            dma((chunks,)), dma((chunks,)),
            dma((2, 2, chunks)), dma((2, 2, chunks)),
            dma((2, 2, chunks)), dma((2, 2, chunks)),
            dma((stages,)), dma((stages,)),
        ],
        compiler_params=pltpu.CompilerParams(collective_id=0, has_side_effects=True, vmem_limit_bytes=52 << 20),
        name="forecast",
    )(ocean_status, height_driver, flat(obs_index, -1), flat(obs_value, 0), flat(obs_error, 1))
    return pl.pallas_call(
        analysis_kernel,
        grid=(fields,),
        out_shape=jax.ShapeDtypeStruct(ocean_status.shape, f32),
        in_specs=[pl.BlockSpec((members + 8, members), lambda i: (0, 0)),
                  pl.BlockSpec((chunks, 1, rows, CHUNK, width), lambda i: (0, i, 0, 0, 0))],
        out_specs=pl.BlockSpec((members, 1, rows, width), lambda i: (0, i, 0, 0)),
        scratch_shapes=[pltpu.VMEM((2 * members, 2 * members), jnp.bfloat16)],
        compiler_params=pltpu.CompilerParams(vmem_limit_bytes=48 << 20),
        name="analysis",
    )(sums, fore)


def solution(mesh):
    return jax.shard_map(
        functools.partial(shards, mesh.shape["lat"], mesh.shape["lon"]),
        mesh=mesh,
        in_specs=(
            P(None, None, "lat", "lon"),
            P(None, "lat", "lon"),
            P("lat", "lon", None),
            P("lat", "lon", None),
            P("lat", "lon", None),
        ),
        out_specs=P(None, None, "lat", "lon"),
        check_vma=False,
    )
```

```python
import functools
import math

import jax
import jax.numpy as jnp
from jax import lax
from jax.experimental import pallas as pl
from jax.experimental.pallas import tpu as pltpu
from jax.sharding import PartitionSpec as P

NS_ITERS = 14
COURANT = 0.2
DIFFUSION = 0.1
FORCE_STEP = 0.5
CORIOLIS_MAX = 0.3
CHUNK = 16
LANES = 128
MESH = pl.DeviceIdType.MESH


def doublings(count):
    return [1 << b for b in range(count.bit_length() - 1)]


def parts_of(x, count):
    parts = []
    for _ in range(count):
        parts.append(x.astype(jnp.bfloat16))
        x = x - parts[-1].astype(jnp.float32)
    return parts


def product(a, b):
    rows, columns = a.shape[0], b.shape[1]
    whole = jnp.dot(jnp.concatenate(parts_of(a, 2), axis=0), jnp.concatenate(parts_of(b, 2), axis=1),
                    preferred_element_type=jnp.float32)
    return (whole[:rows, :columns] + whole[:rows, columns:]) + (whole[rows:, :columns] + whole[rows:, columns:])


def paired(a, b):
    columns = b.shape[1]
    terms = jnp.concatenate(parts_of(b, 2), axis=1)
    whole = jnp.dot(jnp.concatenate(parts_of(a, 2), axis=1), jnp.concatenate([terms, terms], axis=0),
                    preferred_element_type=jnp.float32)
    return whole[:, :columns] + whole[:, columns:]


def fold(sums):
    members = sums.shape[1]
    half = members // 2
    row = lax.broadcasted_iota(jnp.int32, (half, members), 0)
    column = lax.broadcasted_iota(jnp.int32, (half, members), 1)
    corner = pltpu.roll(sums[half:members], half, 1)
    mixed = jnp.where((column < half) & (row > column), corner, sums[:half])
    diagonal = jnp.sum(jnp.where(row == column, corner, 0.0), axis=0, keepdims=True)
    place = lax.broadcasted_iota(jnp.int32, (8, members), 0)
    return jnp.concatenate([mixed, jnp.where(place == 0, sums[members:], diagonal)], axis=0)


def unfold(folded):
    half = folded.shape[0] - 8
    members = 2 * half
    row = lax.broadcasted_iota(jnp.int32, (members, members), 0)
    column = lax.broadcasted_iota(jnp.int32, (members, members), 1)
    upper = jnp.concatenate([folded[:half], jnp.zeros((half, members), jnp.float32)], axis=0)
    lower = pltpu.roll(pltpu.roll(upper, half, 0), half, 1)
    diagonal = pltpu.roll(folded[half:], half, 1)[1:2]
    first = jnp.where((column >= half) | (row <= column), upper, upper.T)
    last = jnp.where(column < half, upper.T,
                     jnp.where(row > column, lower, jnp.where(row < column, lower.T, diagonal)))
    return jnp.where(row < half, first, last)


def forecast_kernel(n_lat, n_lon, state_hbm, force_hbm, index_ref, value_ref, error_ref, fore_hbm, sums_ref,
                    raw, force, ext, cols_out, cols_in, fore, onehot, readings, acc, acc_in,
                    in_sem, force_sem, out_sem, row_send, row_recv, col_send, col_recv, sum_send, sum_recv):
    chunks = raw.shape[0]
    members = chunks * CHUNK
    sites = index_ref.shape[-1]
    rows, width = raw.shape[3], raw.shape[4]
    lat, lon = lax.axis_index("lat"), lax.axis_index("lon")
    east = (lat, lax.rem(lon + 1, n_lon))
    west = (lat, lax.rem(lon + n_lon - 1, n_lon))
    has_south, has_north = lat > 0, lat < n_lat - 1
    south, north = (jnp.maximum(lat - 1, 0), lon), (jnp.minimum(lat + 1, n_lat - 1), lon)

    def dev(place):
        return {"lat": place[0], "lon": place[1]}

    partners = [(lat, lon ^ d) for d in doublings(n_lon)] + [(lat ^ d, lon) for d in doublings(n_lat)]
    far = [(lat, lon ^ d) for d in doublings(n_lon)[1:]] + [(lat ^ d, lon) for d in doublings(n_lat)[1:]]

    def load(c):
        return pltpu.make_async_copy(state_hbm.at[pl.ds(c * CHUNK, CHUNK)], raw.at[c], in_sem.at[c])

    def load_force(c):
        return pltpu.make_async_copy(force_hbm.at[pl.ds(c * CHUNK, CHUNK)], force.at[c], force_sem.at[c])

    @pl.loop(0, chunks)
    def _(c):
        load(c).start()
        load_force(c).start()

    barrier = pltpu.get_barrier_semaphore()
    for place in [east, west] + far:
        pl.semaphore_signal(barrier, inc=1, device_id=dev(place), device_id_type=MESH)

    @pl.when(has_south)
    def _():
        pl.semaphore_signal(barrier, inc=1, device_id=dev(south), device_id_type=MESH)

    @pl.when(has_north)
    def _():
        pl.semaphore_signal(barrier, inc=1, device_id=dev(north), device_id_type=MESH)

    pl.semaphore_wait(barrier, 2 + len(far) + has_south.astype(jnp.int32) + has_north.astype(jnp.int32))

    def row_copy(step, c, side):
        return pltpu.make_async_remote_copy(
            src_ref=ext.at[step, c, :, rows if side == 0 else 1],
            dst_ref=ext.at[step, c, :, 0 if side == 0 else rows + 1],
            send_sem=row_send.at[step, side, c], recv_sem=row_recv.at[step, side, c],
            device_id=dev(north if side == 0 else south), device_id_type=MESH)

    def col_copy(step, c, side):
        return pltpu.make_async_remote_copy(
            src_ref=cols_out.at[step, side, c], dst_ref=cols_in.at[step, side, c],
            send_sem=col_send.at[step, side, c], recv_sem=col_recv.at[step, side, c],
            device_id=dev(east if side == 0 else west), device_id_type=MESH)

    lane = lax.broadcasted_iota(jnp.int32, (CHUNK, LANES), 1)
    wide = lax.broadcasted_iota(jnp.int32, (CHUNK, width), 1)

    def send(step, c):
        @pl.when(has_north)
        def _():
            row_copy(step, c, 0).start()

        @pl.when(has_south)
        def _():
            row_copy(step, c, 1).start()

        last = jnp.zeros((CHUNK, LANES), jnp.float32)
        first = last
        for f in range(3):
            for r in range(rows):
                j = f * rows + r
                last = jnp.where(lane == j, ext[step, c, f, r + 1, :, width - 1:width], last)
                first = jnp.where(lane == j, ext[step, c, f, r + 1, :, 0:1], first)
        cols_out[step, 0, c] = last
        cols_out[step, 1, c] = first
        col_copy(step, c, 0).start()
        col_copy(step, c, 1).start()

    def receive(step, c):
        @pl.when(has_south)
        def _():
            row_copy(step, c, 0).wait_recv()

        @pl.when(has_north)
        def _():
            row_copy(step, c, 1).wait_recv()

        col_copy(step, c, 0).wait_recv()
        col_copy(step, c, 1).wait_recv()

    @pl.when(lat == 0)
    def _():
        for step in range(2):
            @pl.loop(0, chunks)
            def _(c):
                ext[step, c, :, 0] = jnp.zeros((3, CHUNK, width), jnp.float32)

    @pl.when(lat == n_lat - 1)
    def _():
        for step in range(2):
            @pl.loop(0, chunks)
            def _(c):
                ext[step, c, :, rows + 1] = jnp.zeros((3, CHUNK, width), jnp.float32)

    @pl.loop(0, chunks)
    def _(c):
        load(c).wait()
        for f in range(3):
            ext[0, c, f, pl.ds(1, rows)] = jnp.swapaxes(raw[c, :, f], 0, 1)
        send(0, c)

    total_rows = float(n_lat * rows)
    first_row = (lat * rows).astype(jnp.float32)

    def advance(step, c, put):
        pushes = jnp.swapaxes(force[c].astype(jnp.float32), 0, 1)
        from_west = cols_in[step, 0, c]
        from_east = cols_in[step, 1, c]
        for r in range(rows):
            coriolis = CORIOLIS_MAX * (2.0 * (first_row + (r + 0.5)) / total_rows - 1.0)

            def around(f):
                mid = ext[step, c, f, r + 1]
                j = f * rows + r
                e = jnp.where(wide == width - 1, from_east[:, j:j + 1], pltpu.roll(mid, width - 1, 1))
                w = jnp.where(wide == 0, from_west[:, j:j + 1], pltpu.roll(mid, 1, 1))
                return mid, e, w, ext[step, c, f, r + 2], ext[step, c, f, r]

            h, he, hw, hn, hs = around(0)
            u, ue, uw, un, us = around(1)
            v, ve, vw, vn, vs = around(2)
            half = 0.5 * COURANT
            h_new = (h - half * (((1.0 + he) * ue - (1.0 + hw) * uw) + ((1.0 + hn) * vn - (1.0 + hs) * vs))
                     + DIFFUSION * (he + hw + hn + hs - 4.0 * h) + FORCE_STEP * pushes[r])
            u_new = (u - half * ((he - hw) + u * (ue - uw) + v * (un - us))
                     + COURANT * coriolis * v + DIFFUSION * (ue + uw + un + us - 4.0 * u))
            v_new = (v - half * ((hn - hs) + u * (ve - vw) + v * (vn - vs))
                     - COURANT * coriolis * u + DIFFUSION * (ve + vw + vn + vs - 4.0 * v))
            put(r, h_new, u_new, v_new)

    @pl.loop(0, chunks)
    def _(c):
        receive(0, c)
        load_force(c).wait()

        def put(r, *new):
            for f in range(3):
                ext[1, c, f, r + 1] = new[f]

        advance(0, c, put)
        send(1, c)

    for r in range(rows):
        cell = lax.broadcasted_iota(jnp.int32, (width, sites), 0) + r * width
        onehot[r] = jnp.where(cell == index_ref[0], 1.0, 0.0).astype(jnp.bfloat16)

    def save(c):
        return pltpu.make_async_copy(fore.at[c], fore_hbm.at[c], out_sem.at[c])

    @pl.loop(0, chunks)
    def _(c):
        receive(1, c)

        def put(r, *new):
            for f in range(3):
                fore[c, f, r] = new[f]

        advance(1, c, put)
        save(c).start()
        seen = jnp.zeros((CHUNK, sites), jnp.float32)
        for r in range(rows):
            picked = jnp.dot(jnp.concatenate(parts_of(fore[c, 0, r], 3), axis=0), onehot[r],
                             preferred_element_type=jnp.float32)
            seen += (picked[:CHUNK] + picked[CHUNK:2 * CHUNK]) + picked[2 * CHUNK:]
        readings[c] = seen

    seen = readings[...].reshape(members, sites)
    mean = jnp.mean(seen, axis=0, keepdims=True)
    spread = seen - mean
    inv = 1.0 / error_ref[0]
    innovation = inv * (value_ref[0] - mean)
    left = jnp.concatenate([spread * inv, jnp.broadcast_to(innovation, (8, sites))], axis=0)
    acc[0] = fold(product(left, spread.T))
    swaps = [pltpu.make_async_remote_copy(
        src_ref=acc.at[s], dst_ref=acc_in.at[s], send_sem=sum_send.at[s], recv_sem=sum_recv.at[s],
        device_id=dev(place), device_id_type=MESH) for s, place in enumerate(partners)]
    for s, swap in enumerate(swaps):
        swap.start()
        swap.wait_recv()
        acc[s + 1] = acc[s] + acc_in[s]
    sums_ref[...] = acc[len(swaps)]
    for swap in swaps:
        swap.wait_send()

    @pl.loop(0, chunks)
    def _(c):
        save(c).wait()
        for step in range(2):
            @pl.when(has_north)
            def _():
                row_copy(step, c, 0).wait_send()

            @pl.when(has_south)
            def _():
                row_copy(step, c, 1).wait_send()

            col_copy(step, c, 0).wait_send()
            col_copy(step, c, 1).wait_send()


def analysis_kernel(sums_ref, fore_ref, out_ref, mix):
    members = sums_ref.shape[1]
    half = members // 2
    rows = fore_ref.shape[2]
    width = fore_ref.shape[4]

    @pl.when(pl.program_id(0) == 0)
    def _():
        eye = (lax.broadcasted_iota(jnp.int32, (members, members), 0)
               == lax.broadcasted_iota(jnp.int32, (members, members), 1)).astype(jnp.float32)
        amat = (members - 1) * eye + unfold(sums_ref[...])
        scale = jnp.sqrt(jnp.sum(jnp.sum(amat * amat, axis=1, keepdims=True), axis=0, keepdims=True))

        def turn(_, pair):
            upper, lower = pair
            factor = 1.5 * eye - 0.5 * paired(lower, upper)
            both = paired(jnp.concatenate([upper, lower], axis=0), factor)
            return both[:members], both[members:]

        upper = amat / scale
        lower = 1.5 * eye - 0.5 * upper
        upper = paired(upper, lower)
        upper, lower = lax.fori_loop(1, NS_ITERS - 1, turn, (upper, lower))
        lower = paired(lower, 1.5 * eye - 0.5 * paired(lower, upper))
        root = lower / jnp.sqrt(scale)
        inverse = paired(root, root)
        shift = paired(sums_ref[half:], inverse.T)
        weights = math.sqrt(members - 1) * root.T + shift[0:1, :]
        high = weights.astype(jnp.bfloat16)
        low = (weights - high.astype(jnp.float32)).astype(jnp.bfloat16)
        mix[:members, :members] = high
        mix[:members, members:] = high
        mix[members:, :members] = low
        mix[members:, members:] = jnp.zeros_like(low)

    for r in range(rows):
        cells = fore_ref[:, 0, r].reshape(members, width)
        mean = jnp.mean(cells, axis=0, keepdims=True)
        spread = cells - mean
        high = spread.astype(jnp.bfloat16)
        low = (spread - high.astype(jnp.float32)).astype(jnp.bfloat16)
        both = jnp.dot(mix[...], jnp.concatenate([high, low], axis=0), preferred_element_type=jnp.float32)
        out_ref[:, 0, r, :] = mean + both[:members] + both[members:]


def shards(n_lat, n_lon, ocean_status, height_driver, obs_index, obs_value, obs_error):
    members, fields, rows, width = ocean_status.shape
    chunks = members // CHUNK
    sites = obs_index.shape[-1]
    vmem = pl.BlockSpec(memory_space=pltpu.VMEM)
    anywhere = pl.BlockSpec(memory_space=pl.ANY)
    stages = len(doublings(n_lon)) + len(doublings(n_lat))
    dma = pltpu.SemaphoreType.DMA
    f32 = jnp.float32
    block = (chunks, fields, rows, CHUNK, width)
    fore, sums = pl.pallas_call(
        functools.partial(forecast_kernel, n_lat, n_lon),
        out_shape=(jax.ShapeDtypeStruct(block, f32), jax.ShapeDtypeStruct((members // 2 + 8, members), f32)),
        in_specs=[anywhere, anywhere, vmem, vmem, vmem],
        out_specs=(anywhere, vmem),
        scratch_shapes=[
            pltpu.VMEM((chunks, CHUNK, fields, rows, width), f32),
            pltpu.VMEM((chunks, CHUNK, rows, width), height_driver.dtype),
            pltpu.VMEM((2, chunks, fields, rows + 2, CHUNK, width), f32),
            pltpu.VMEM((2, 2, chunks, CHUNK, LANES), f32),
            pltpu.VMEM((2, 2, chunks, CHUNK, LANES), f32),
            pltpu.VMEM(block, f32),
            pltpu.VMEM((rows, width, sites), jnp.bfloat16),
            pltpu.VMEM((chunks, CHUNK, sites), f32),
            pltpu.VMEM((stages + 1, members // 2 + 8, members), f32),
            pltpu.VMEM((stages, members // 2 + 8, members), f32),
            dma((chunks,)), dma((chunks,)), dma((chunks,)),
            dma((2, 2, chunks)), dma((2, 2, chunks)),
            dma((2, 2, chunks)), dma((2, 2, chunks)),
            dma((stages,)), dma((stages,)),
        ],
        compiler_params=pltpu.CompilerParams(collective_id=0, has_side_effects=True, vmem_limit_bytes=63 << 20),
        name="forecast",
    )(ocean_status, height_driver, obs_index, obs_value, obs_error)
    return pl.pallas_call(
        analysis_kernel,
        grid=(fields,),
        out_shape=jax.ShapeDtypeStruct(ocean_status.shape, f32),
        in_specs=[pl.BlockSpec((members // 2 + 8, members), lambda i: (0, 0)),
                  pl.BlockSpec((chunks, 1, rows, CHUNK, width), lambda i: (0, i, 0, 0, 0))],
        out_specs=pl.BlockSpec((members, 1, rows, width), lambda i: (0, i, 0, 0)),
        scratch_shapes=[pltpu.VMEM((2 * members, 2 * members), jnp.bfloat16)],
        compiler_params=pltpu.CompilerParams(vmem_limit_bytes=63 << 20),
        name="analysis",
    )(sums, fore)


def solution(mesh):
    return jax.shard_map(
        functools.partial(shards, mesh.shape["lat"], mesh.shape["lon"]),
        mesh=mesh,
        in_specs=(
            P(None, None, "lat", "lon"),
            P(None, "lat", "lon"),
            P("lat", "lon", None),
            P("lat", "lon", None),
            P("lat", "lon", None),
        ),
        out_specs=P(None, None, "lat", "lon"),
        check_vma=False,
    )
```

```python
import functools
import math

import jax
import jax.numpy as jnp
from jax import lax
from jax.experimental import pallas as pl
from jax.experimental.pallas import tpu as pltpu
from jax.sharding import PartitionSpec as P

NS_ITERS = 14
COURANT = 0.2
DIFFUSION = 0.1
FORCE_STEP = 0.5
CORIOLIS_MAX = 0.3
CHUNK = 16
LANES = 128
MESH = pl.DeviceIdType.MESH


def doublings(count):
    return [1 << b for b in range(count.bit_length() - 1)]


def parts_of(x, count):
    parts = []
    for _ in range(count):
        parts.append(x.astype(jnp.bfloat16))
        x = x - parts[-1].astype(jnp.float32)
    return parts


def product(a, b):
    rows, columns = a.shape[0], b.shape[1]
    whole = jnp.dot(jnp.concatenate(parts_of(a, 2), axis=0), jnp.concatenate(parts_of(b, 2), axis=1),
                    preferred_element_type=jnp.float32)
    return (whole[:rows, :columns] + whole[:rows, columns:]) + (whole[rows:, :columns] + whole[rows:, columns:])


def paired(a, b):
    columns = b.shape[1]
    terms = jnp.concatenate(parts_of(b, 2), axis=1)
    whole = jnp.dot(jnp.concatenate(parts_of(a, 2), axis=1), jnp.concatenate([terms, terms], axis=0),
                    preferred_element_type=jnp.float32)
    return whole[:, :columns] + whole[:, columns:]


def fold(sums):
    members = sums.shape[1]
    half = members // 2
    row = lax.broadcasted_iota(jnp.int32, (half, members), 0)
    column = lax.broadcasted_iota(jnp.int32, (half, members), 1)
    corner = pltpu.roll(sums[half:members], half, 1)
    mixed = jnp.where((column < half) & (row > column), corner, sums[:half])
    diagonal = jnp.sum(jnp.where(row == column, corner, 0.0), axis=0, keepdims=True)
    place = lax.broadcasted_iota(jnp.int32, (8, members), 0)
    return jnp.concatenate([mixed, jnp.where(place == 0, sums[members:], diagonal)], axis=0)


def unfold(folded):
    half = folded.shape[0] - 8
    members = 2 * half
    row = lax.broadcasted_iota(jnp.int32, (members, members), 0)
    column = lax.broadcasted_iota(jnp.int32, (members, members), 1)
    upper = jnp.concatenate([folded[:half], jnp.zeros((half, members), jnp.float32)], axis=0)
    lower = pltpu.roll(pltpu.roll(upper, half, 0), half, 1)
    diagonal = pltpu.roll(folded[half:], half, 1)[1:2]
    first = jnp.where((column >= half) | (row <= column), upper, upper.T)
    last = jnp.where(column < half, upper.T,
                     jnp.where(row > column, lower, jnp.where(row < column, lower.T, diagonal)))
    return jnp.where(row < half, first, last)


def forecast_kernel(n_lat, n_lon, state_hbm, force_hbm, index_ref, value_ref, error_ref, fore_hbm, sums_ref,
                    raw, force, ext, relay, cols_out, cols_in, fore, onehot, readings, acc, acc_in,
                    in_sem, force_sem, out_sem, row_send, row_recv, relay_recv, relay_send, col_send, col_recv, sum_send, sum_recv):
    chunks = raw.shape[0]
    members = chunks * CHUNK
    sites = index_ref.shape[-1]
    rows, width = raw.shape[3], raw.shape[4]
    lat, lon = lax.axis_index("lat"), lax.axis_index("lon")
    east = (lat, lax.rem(lon + 1, n_lon))
    west = (lat, lax.rem(lon + n_lon - 1, n_lon))
    has_south, has_north = lat > 0, lat < n_lat - 1
    south, north = (jnp.maximum(lat - 1, 0), lon), (jnp.minimum(lat + 1, n_lat - 1), lon)

    planes = n_lat // 2
    parity = lax.rem(lat, 2)
    plane = lat // 2
    detours_out = chunks * (parity * (planes - 1 - plane) + (1 - parity) * plane) // planes
    detours_by = chunks * ((1 - parity) * (planes - 1 - plane) + parity * plane) // planes

    def detoured(c, count):
        return lax.rem((chunks - 1 - c) * count, chunks) >= chunks - count

    def dev(place):
        return {"lat": place[0], "lon": place[1]}

    partners = [(lat, lon ^ d) for d in doublings(n_lon)] + [(lat ^ d, lon) for d in doublings(n_lat)]
    far = [(lat, lon ^ d) for d in doublings(n_lon)[1:]] + [(lat ^ d, lon) for d in doublings(n_lat)[1:]]

    def load(c):
        return pltpu.make_async_copy(state_hbm.at[pl.ds(c * CHUNK, CHUNK)], raw.at[c], in_sem.at[c])

    def load_force(c):
        return pltpu.make_async_copy(force_hbm.at[pl.ds(c * CHUNK, CHUNK)], force.at[c], force_sem.at[c])

    @pl.loop(0, chunks)
    def _(c):
        load(c).start()
        load_force(c).start()

    barrier = pltpu.get_barrier_semaphore()
    for place in [east, west] + far:
        pl.semaphore_signal(barrier, inc=1, device_id=dev(place), device_id_type=MESH)

    @pl.when(has_south)
    def _():
        pl.semaphore_signal(barrier, inc=1, device_id=dev(south), device_id_type=MESH)

    @pl.when(has_north)
    def _():
        pl.semaphore_signal(barrier, inc=1, device_id=dev(north), device_id_type=MESH)

    @pl.when(lat > 1)
    def _():
        pl.semaphore_signal(barrier, inc=1, device_id=dev((jnp.maximum(lat - 2, 0), lon)), device_id_type=MESH)

    @pl.when(lat < n_lat - 2)
    def _():
        pl.semaphore_signal(barrier, inc=1, device_id=dev((jnp.minimum(lat + 2, n_lat - 1), lon)), device_id_type=MESH)

    present = [has_south, has_north, lat > 1, lat < n_lat - 2]
    pl.semaphore_wait(barrier, 2 + len(far) + sum(there.astype(jnp.int32) for there in present))

    def row_copy(step, c, side):
        return pltpu.make_async_remote_copy(
            src_ref=ext.at[step, c, :, rows if side == 0 else 1],
            dst_ref=ext.at[step, c, :, 0 if side == 0 else rows + 1],
            send_sem=row_send.at[step, side, c], recv_sem=row_recv.at[step, side, c],
            device_id=dev(north if side == 0 else south), device_id_type=MESH)

    def detour_copy(step, c):
        return pltpu.make_async_remote_copy(
            src_ref=ext.at[step, c, :, 1 + (rows - 1) * parity], dst_ref=relay.at[step, c],
            send_sem=row_send.at[step, 1 - parity, c], recv_sem=relay_recv.at[step, c],
            device_id=dev((lat + 1 - 2 * parity, lon)), device_id_type=MESH)

    def onward_copy(step, c):
        return pltpu.make_async_remote_copy(
            src_ref=relay.at[step, c], dst_ref=ext.at[step, c, :, (rows + 1) * parity],
            send_sem=relay_send.at[step, c], recv_sem=row_recv.at[step, parity, c],
            device_id=dev((jnp.clip(lat + 2 - 4 * parity, 0, n_lat - 1), lon)), device_id_type=MESH)

    def hand_on(step, c):
        @pl.when(detoured(c, detours_by))
        def _():
            detour_copy(step, c).wait_recv()
            onward_copy(step, c).start()

    def col_copy(step, c, side):
        return pltpu.make_async_remote_copy(
            src_ref=cols_out.at[step, side, c], dst_ref=cols_in.at[step, side, c],
            send_sem=col_send.at[step, side, c], recv_sem=col_recv.at[step, side, c],
            device_id=dev(east if side == 0 else west), device_id_type=MESH)

    lane = lax.broadcasted_iota(jnp.int32, (CHUNK, LANES), 1)
    wide = lax.broadcasted_iota(jnp.int32, (CHUNK, width), 1)

    def send(step, c):
        by = detoured(c, detours_out)

        @pl.when(by)
        def _():
            detour_copy(step, c).start()

        @pl.when(has_north & jnp.logical_not(by & (parity == 1)))
        def _():
            row_copy(step, c, 0).start()

        @pl.when(has_south & jnp.logical_not(by & (parity == 0)))
        def _():
            row_copy(step, c, 1).start()

        last = jnp.zeros((CHUNK, LANES), jnp.float32)
        first = last
        for f in range(3):
            for r in range(rows):
                j = f * rows + r
                last = jnp.where(lane == j, ext[step, c, f, r + 1, :, width - 1:width], last)
                first = jnp.where(lane == j, ext[step, c, f, r + 1, :, 0:1], first)
        cols_out[step, 0, c] = last
        cols_out[step, 1, c] = first
        col_copy(step, c, 0).start()
        col_copy(step, c, 1).start()

    def receive(step, c):
        @pl.when(has_south)
        def _():
            row_copy(step, c, 0).wait_recv()

        @pl.when(has_north)
        def _():
            row_copy(step, c, 1).wait_recv()

        col_copy(step, c, 0).wait_recv()
        col_copy(step, c, 1).wait_recv()

    @pl.when(lat == 0)
    def _():
        for step in range(2):
            @pl.loop(0, chunks)
            def _(c):
                ext[step, c, :, 0] = jnp.zeros((3, CHUNK, width), jnp.float32)

    @pl.when(lat == n_lat - 1)
    def _():
        for step in range(2):
            @pl.loop(0, chunks)
            def _(c):
                ext[step, c, :, rows + 1] = jnp.zeros((3, CHUNK, width), jnp.float32)

    @pl.loop(0, chunks)
    def _(c):
        load(c).wait()
        for f in range(3):
            ext[0, c, f, pl.ds(1, rows)] = jnp.swapaxes(raw[c, :, f], 0, 1)
        send(0, c)

    total_rows = float(n_lat * rows)
    first_row = (lat * rows).astype(jnp.float32)

    def advance(step, c, put):
        pushes = jnp.swapaxes(force[c].astype(jnp.float32), 0, 1)
        from_west = cols_in[step, 0, c]
        from_east = cols_in[step, 1, c]
        for r in range(rows):
            coriolis = CORIOLIS_MAX * (2.0 * (first_row + (r + 0.5)) / total_rows - 1.0)

            def around(f):
                mid = ext[step, c, f, r + 1]
                j = f * rows + r
                e = jnp.where(wide == width - 1, from_east[:, j:j + 1], pltpu.roll(mid, width - 1, 1))
                w = jnp.where(wide == 0, from_west[:, j:j + 1], pltpu.roll(mid, 1, 1))
                return mid, e, w, ext[step, c, f, r + 2], ext[step, c, f, r]

            h, he, hw, hn, hs = around(0)
            u, ue, uw, un, us = around(1)
            v, ve, vw, vn, vs = around(2)
            half = 0.5 * COURANT
            h_new = (h - half * (((1.0 + he) * ue - (1.0 + hw) * uw) + ((1.0 + hn) * vn - (1.0 + hs) * vs))
                     + DIFFUSION * (he + hw + hn + hs - 4.0 * h) + FORCE_STEP * pushes[r])
            u_new = (u - half * ((he - hw) + u * (ue - uw) + v * (un - us))
                     + COURANT * coriolis * v + DIFFUSION * (ue + uw + un + us - 4.0 * u))
            v_new = (v - half * ((hn - hs) + u * (ve - vw) + v * (vn - vs))
                     - COURANT * coriolis * u + DIFFUSION * (ve + vw + vn + vs - 4.0 * v))
            put(r, h_new, u_new, v_new)

    @pl.loop(0, chunks)
    def _(c):
        hand_on(0, c)
        receive(0, c)
        load_force(c).wait()

        def put(r, *new):
            for f in range(3):
                ext[1, c, f, r + 1] = new[f]

        advance(0, c, put)
        send(1, c)

    for r in range(rows):
        cell = lax.broadcasted_iota(jnp.int32, (width, sites), 0) + r * width
        onehot[r] = jnp.where(cell == index_ref[0], 1.0, 0.0).astype(jnp.bfloat16)

    def save(c):
        return pltpu.make_async_copy(fore.at[c], fore_hbm.at[c], out_sem.at[c])

    @pl.loop(0, chunks)
    def _(c):
        hand_on(1, c)
        receive(1, c)

        def put(r, *new):
            for f in range(3):
                fore[c, f, r] = new[f]

        advance(1, c, put)
        save(c).start()
        seen = jnp.zeros((CHUNK, sites), jnp.float32)
        for r in range(rows):
            picked = jnp.dot(jnp.concatenate(parts_of(fore[c, 0, r], 3), axis=0), onehot[r],
                             preferred_element_type=jnp.float32)
            seen += (picked[:CHUNK] + picked[CHUNK:2 * CHUNK]) + picked[2 * CHUNK:]
        readings[c] = seen

    seen = readings[...].reshape(members, sites)
    mean = jnp.mean(seen, axis=0, keepdims=True)
    spread = seen - mean
    inv = 1.0 / error_ref[0]
    innovation = inv * (value_ref[0] - mean)
    left = jnp.concatenate([spread * inv, jnp.broadcast_to(innovation, (8, sites))], axis=0)
    acc[0] = fold(product(left, spread.T))
    swaps = [pltpu.make_async_remote_copy(
        src_ref=acc.at[s], dst_ref=acc_in.at[s], send_sem=sum_send.at[s], recv_sem=sum_recv.at[s],
        device_id=dev(place), device_id_type=MESH) for s, place in enumerate(partners)]
    for s, swap in enumerate(swaps):
        swap.start()
        swap.wait_recv()
        acc[s + 1] = acc[s] + acc_in[s]
    sums_ref[...] = acc[len(swaps)]
    for swap in swaps:
        swap.wait_send()

    @pl.loop(0, chunks)
    def _(c):
        save(c).wait()
        for step in range(2):
            @pl.when(has_north)
            def _():
                row_copy(step, c, 0).wait_send()

            @pl.when(has_south)
            def _():
                row_copy(step, c, 1).wait_send()

            @pl.when(detoured(c, detours_by))
            def _():
                onward_copy(step, c).wait_send()

            col_copy(step, c, 0).wait_send()
            col_copy(step, c, 1).wait_send()


def analysis_kernel(sums_ref, fore_ref, out_ref, mix):
    members = sums_ref.shape[1]
    half = members // 2
    rows = fore_ref.shape[2]
    width = fore_ref.shape[4]

    @pl.when(pl.program_id(0) == 0)
    def _():
        eye = (lax.broadcasted_iota(jnp.int32, (members, members), 0)
               == lax.broadcasted_iota(jnp.int32, (members, members), 1)).astype(jnp.float32)
        amat = (members - 1) * eye + unfold(sums_ref[...])
        scale = jnp.sqrt(jnp.sum(jnp.sum(amat * amat, axis=1, keepdims=True), axis=0, keepdims=True))

        def turn(_, pair):
            upper, lower = pair
            factor = 1.5 * eye - 0.5 * paired(lower, upper)
            both = paired(jnp.concatenate([upper, lower], axis=0), factor)
            return both[:members], both[members:]

        upper = amat / scale
        lower = 1.5 * eye - 0.5 * upper
        upper = paired(upper, lower)
        upper, lower = lax.fori_loop(1, NS_ITERS - 1, turn, (upper, lower))
        lower = paired(lower, 1.5 * eye - 0.5 * paired(lower, upper))
        root = lower / jnp.sqrt(scale)
        inverse = paired(root, root)
        shift = paired(sums_ref[half:], inverse.T)
        weights = math.sqrt(members - 1) * root.T + shift[0:1, :]
        high = weights.astype(jnp.bfloat16)
        low = (weights - high.astype(jnp.float32)).astype(jnp.bfloat16)
        mix[:members, :members] = high
        mix[:members, members:] = high
        mix[members:, :members] = low
        mix[members:, members:] = jnp.zeros_like(low)

    for r in range(rows):
        cells = fore_ref[:, 0, r].reshape(members, width)
        mean = jnp.mean(cells, axis=0, keepdims=True)
        spread = cells - mean
        high = spread.astype(jnp.bfloat16)
        low = (spread - high.astype(jnp.float32)).astype(jnp.bfloat16)
        both = jnp.dot(mix[...], jnp.concatenate([high, low], axis=0), preferred_element_type=jnp.float32)
        out_ref[:, 0, r, :] = mean + both[:members] + both[members:]


def shards(n_lat, n_lon, ocean_status, height_driver, obs_index, obs_value, obs_error):
    members, fields, rows, width = ocean_status.shape
    chunks = members // CHUNK
    sites = obs_index.shape[-1]
    vmem = pl.BlockSpec(memory_space=pltpu.VMEM)
    anywhere = pl.BlockSpec(memory_space=pl.ANY)
    stages = len(doublings(n_lon)) + len(doublings(n_lat))
    dma = pltpu.SemaphoreType.DMA
    f32 = jnp.float32
    block = (chunks, fields, rows, CHUNK, width)
    fore, sums = pl.pallas_call(
        functools.partial(forecast_kernel, n_lat, n_lon),
        out_shape=(jax.ShapeDtypeStruct(block, f32), jax.ShapeDtypeStruct((members // 2 + 8, members), f32)),
        in_specs=[anywhere, anywhere, vmem, vmem, vmem],
        out_specs=(anywhere, vmem),
        scratch_shapes=[
            pltpu.VMEM((chunks, CHUNK, fields, rows, width), f32),
            pltpu.VMEM((chunks, CHUNK, rows, width), height_driver.dtype),
            pltpu.VMEM((2, chunks, fields, rows + 2, CHUNK, width), f32),
            pltpu.VMEM((2, chunks, fields, CHUNK, width), f32),
            pltpu.VMEM((2, 2, chunks, CHUNK, LANES), f32),
            pltpu.VMEM((2, 2, chunks, CHUNK, LANES), f32),
            pltpu.VMEM(block, f32),
            pltpu.VMEM((rows, width, sites), jnp.bfloat16),
            pltpu.VMEM((chunks, CHUNK, sites), f32),
            pltpu.VMEM((stages + 1, members // 2 + 8, members), f32),
            pltpu.VMEM((stages, members // 2 + 8, members), f32),
            dma((chunks,)), dma((chunks,)), dma((chunks,)),
            dma((2, 2, chunks)), dma((2, 2, chunks)),
            dma((2, chunks)), dma((2, chunks)),
            dma((2, 2, chunks)), dma((2, 2, chunks)),
            dma((stages,)), dma((stages,)),
        ],
        compiler_params=pltpu.CompilerParams(collective_id=0, has_side_effects=True, vmem_limit_bytes=63 << 20),
        name="forecast",
    )(ocean_status, height_driver, obs_index, obs_value, obs_error)
    return pl.pallas_call(
        analysis_kernel,
        grid=(fields,),
        out_shape=jax.ShapeDtypeStruct(ocean_status.shape, f32),
        in_specs=[pl.BlockSpec((members // 2 + 8, members), lambda i: (0, 0)),
                  pl.BlockSpec((chunks, 1, rows, CHUNK, width), lambda i: (0, i, 0, 0, 0))],
        out_specs=pl.BlockSpec((members, 1, rows, width), lambda i: (0, i, 0, 0)),
        scratch_shapes=[pltpu.VMEM((2 * members, 2 * members), jnp.bfloat16)],
        compiler_params=pltpu.CompilerParams(vmem_limit_bytes=63 << 20),
        name="analysis",
    )(sums, fore)


def solution(mesh):
    return jax.shard_map(
        functools.partial(shards, mesh.shape["lat"], mesh.shape["lon"]),
        mesh=mesh,
        in_specs=(
            P(None, None, "lat", "lon"),
            P(None, "lat", "lon"),
            P("lat", "lon", None),
            P("lat", "lon", None),
            P("lat", "lon", None),
        ),
        out_specs=P(None, None, "lat", "lon"),
        check_vma=False,
    )
```

```python
import functools
import math

import jax
import jax.numpy as jnp
from jax import lax
from jax.experimental import pallas as pl
from jax.experimental.pallas import tpu as pltpu
from jax.sharding import PartitionSpec as P

NS_ITERS = 14
COURANT = 0.2
DIFFUSION = 0.1
FORCE_STEP = 0.5
CORIOLIS_MAX = 0.3
CHUNK = 16
LANES = 128
MESH = pl.DeviceIdType.MESH


def doublings(count):
    return [1 << b for b in range(count.bit_length() - 1)]


def parts_of(x, count):
    parts = []
    for _ in range(count):
        parts.append(x.astype(jnp.bfloat16))
        x = x - parts[-1].astype(jnp.float32)
    return parts


def product(a, b):
    rows, columns = a.shape[0], b.shape[1]
    whole = jnp.dot(jnp.concatenate(parts_of(a, 2), axis=0), jnp.concatenate(parts_of(b, 2), axis=1),
                    preferred_element_type=jnp.float32)
    return (whole[:rows, :columns] + whole[:rows, columns:]) + (whole[rows:, :columns] + whole[rows:, columns:])


def paired(a, b):
    columns = b.shape[1]
    terms = jnp.concatenate(parts_of(b, 2), axis=1)
    whole = jnp.dot(jnp.concatenate(parts_of(a, 2), axis=1), jnp.concatenate([terms, terms], axis=0),
                    preferred_element_type=jnp.float32)
    return whole[:, :columns] + whole[:, columns:]


def fold(sums):
    members = sums.shape[1]
    half = members // 2
    row = lax.broadcasted_iota(jnp.int32, (half, members), 0)
    column = lax.broadcasted_iota(jnp.int32, (half, members), 1)
    corner = pltpu.roll(sums[half:members], half, 1)
    mixed = jnp.where((column < half) & (row > column), corner, sums[:half])
    diagonal = jnp.sum(jnp.where(row == column, corner, 0.0), axis=0, keepdims=True)
    place = lax.broadcasted_iota(jnp.int32, (8, members), 0)
    return jnp.concatenate([mixed, jnp.where(place == 0, sums[members:], diagonal)], axis=0)


def unfold(folded):
    half = folded.shape[0] - 8
    members = 2 * half
    row = lax.broadcasted_iota(jnp.int32, (members, members), 0)
    column = lax.broadcasted_iota(jnp.int32, (members, members), 1)
    upper = jnp.concatenate([folded[:half], jnp.zeros((half, members), jnp.float32)], axis=0)
    lower = pltpu.roll(pltpu.roll(upper, half, 0), half, 1)
    diagonal = pltpu.roll(folded[half:], half, 1)[1:2]
    first = jnp.where((column >= half) | (row <= column), upper, upper.T)
    last = jnp.where(column < half, upper.T,
                     jnp.where(row > column, lower, jnp.where(row < column, lower.T, diagonal)))
    return jnp.where(row < half, first, last)


def forecast_kernel(n_lat, n_lon, state_hbm, force_hbm, index_ref, value_ref, error_ref, terms_hbm, mean_ref, sums_ref,
                    raw, force, ext, relay, cols_out, cols_in, fore, terms, onehot, readings, acc, acc_in,
                    in_sem, force_sem, out_sem, row_send, row_recv, relay_recv, relay_send, col_send, col_recv, sum_send, sum_recv):
    chunks = raw.shape[0]
    members = chunks * CHUNK
    sites = index_ref.shape[-1]
    rows, width = raw.shape[3], raw.shape[4]
    lat, lon = lax.axis_index("lat"), lax.axis_index("lon")
    east = (lat, lax.rem(lon + 1, n_lon))
    west = (lat, lax.rem(lon + n_lon - 1, n_lon))
    has_south, has_north = lat > 0, lat < n_lat - 1
    south, north = (jnp.maximum(lat - 1, 0), lon), (jnp.minimum(lat + 1, n_lat - 1), lon)

    planes = n_lat // 2
    parity = lax.rem(lat, 2)
    plane = lat // 2
    detours_out = chunks * (parity * (planes - 1 - plane) + (1 - parity) * plane) // planes
    detours_by = chunks * ((1 - parity) * (planes - 1 - plane) + parity * plane) // planes

    def detoured(c, count):
        return lax.rem((chunks - 1 - c) * count, chunks) >= chunks - count

    def dev(place):
        return {"lat": place[0], "lon": place[1]}

    partners = [(lat, lon ^ d) for d in doublings(n_lon)] + [(lat ^ d, lon) for d in doublings(n_lat)]
    far = [(lat, lon ^ d) for d in doublings(n_lon)[1:]] + [(lat ^ d, lon) for d in doublings(n_lat)[1:]]

    def load(c):
        return pltpu.make_async_copy(state_hbm.at[pl.ds(c * CHUNK, CHUNK)], raw.at[c], in_sem.at[c])

    def load_force(c):
        return pltpu.make_async_copy(force_hbm.at[pl.ds(c * CHUNK, CHUNK)], force.at[c], force_sem.at[c])

    @pl.loop(0, chunks)
    def _(c):
        load(c).start()
        load_force(c).start()

    barrier = pltpu.get_barrier_semaphore()
    for place in [east, west] + far:
        pl.semaphore_signal(barrier, inc=1, device_id=dev(place), device_id_type=MESH)

    @pl.when(has_south)
    def _():
        pl.semaphore_signal(barrier, inc=1, device_id=dev(south), device_id_type=MESH)

    @pl.when(has_north)
    def _():
        pl.semaphore_signal(barrier, inc=1, device_id=dev(north), device_id_type=MESH)

    @pl.when(lat > 1)
    def _():
        pl.semaphore_signal(barrier, inc=1, device_id=dev((jnp.maximum(lat - 2, 0), lon)), device_id_type=MESH)

    @pl.when(lat < n_lat - 2)
    def _():
        pl.semaphore_signal(barrier, inc=1, device_id=dev((jnp.minimum(lat + 2, n_lat - 1), lon)), device_id_type=MESH)

    present = [has_south, has_north, lat > 1, lat < n_lat - 2]
    pl.semaphore_wait(barrier, 2 + len(far) + sum(there.astype(jnp.int32) for there in present))

    def row_copy(step, c, side):
        return pltpu.make_async_remote_copy(
            src_ref=ext.at[step, c, :, rows if side == 0 else 1],
            dst_ref=ext.at[step, c, :, 0 if side == 0 else rows + 1],
            send_sem=row_send.at[step, side, c], recv_sem=row_recv.at[step, side, c],
            device_id=dev(north if side == 0 else south), device_id_type=MESH)

    def detour_copy(step, c):
        return pltpu.make_async_remote_copy(
            src_ref=ext.at[step, c, :, 1 + (rows - 1) * parity], dst_ref=relay.at[step, c],
            send_sem=row_send.at[step, 1 - parity, c], recv_sem=relay_recv.at[step, c],
            device_id=dev((lat + 1 - 2 * parity, lon)), device_id_type=MESH)

    def onward_copy(step, c):
        return pltpu.make_async_remote_copy(
            src_ref=relay.at[step, c], dst_ref=ext.at[step, c, :, (rows + 1) * parity],
            send_sem=relay_send.at[step, c], recv_sem=row_recv.at[step, parity, c],
            device_id=dev((jnp.clip(lat + 2 - 4 * parity, 0, n_lat - 1), lon)), device_id_type=MESH)

    def hand_on(step, c):
        @pl.when(detoured(c, detours_by))
        def _():
            detour_copy(step, c).wait_recv()
            onward_copy(step, c).start()

    def col_copy(step, c, side):
        return pltpu.make_async_remote_copy(
            src_ref=cols_out.at[step, side, c], dst_ref=cols_in.at[step, side, c],
            send_sem=col_send.at[step, side, c], recv_sem=col_recv.at[step, side, c],
            device_id=dev(east if side == 0 else west), device_id_type=MESH)

    lane = lax.broadcasted_iota(jnp.int32, (CHUNK, LANES), 1)
    wide = lax.broadcasted_iota(jnp.int32, (CHUNK, width), 1)

    def send(step, c):
        by = detoured(c, detours_out)

        @pl.when(by)
        def _():
            detour_copy(step, c).start()

        @pl.when(has_north & jnp.logical_not(by & (parity == 1)))
        def _():
            row_copy(step, c, 0).start()

        @pl.when(has_south & jnp.logical_not(by & (parity == 0)))
        def _():
            row_copy(step, c, 1).start()

        last = jnp.zeros((CHUNK, LANES), jnp.float32)
        first = last
        for f in range(3):
            for r in range(rows):
                j = f * rows + r
                last = jnp.where(lane == j, ext[step, c, f, r + 1, :, width - 1:width], last)
                first = jnp.where(lane == j, ext[step, c, f, r + 1, :, 0:1], first)
        cols_out[step, 0, c] = last
        cols_out[step, 1, c] = first
        col_copy(step, c, 0).start()
        col_copy(step, c, 1).start()

    def receive(step, c):
        @pl.when(has_south)
        def _():
            row_copy(step, c, 0).wait_recv()

        @pl.when(has_north)
        def _():
            row_copy(step, c, 1).wait_recv()

        col_copy(step, c, 0).wait_recv()
        col_copy(step, c, 1).wait_recv()

    @pl.when(lat == 0)
    def _():
        for step in range(2):
            @pl.loop(0, chunks)
            def _(c):
                ext[step, c, :, 0] = jnp.zeros((3, CHUNK, width), jnp.float32)

    @pl.when(lat == n_lat - 1)
    def _():
        for step in range(2):
            @pl.loop(0, chunks)
            def _(c):
                ext[step, c, :, rows + 1] = jnp.zeros((3, CHUNK, width), jnp.float32)

    @pl.loop(0, chunks)
    def _(c):
        load(c).wait()
        for f in range(3):
            ext[0, c, f, pl.ds(1, rows)] = jnp.swapaxes(raw[c, :, f], 0, 1)
        send(0, c)

    total_rows = float(n_lat * rows)
    first_row = (lat * rows).astype(jnp.float32)

    def advance(step, c, put):
        pushes = jnp.swapaxes(force[c].astype(jnp.float32), 0, 1)
        from_west = cols_in[step, 0, c]
        from_east = cols_in[step, 1, c]
        for r in range(rows):
            coriolis = CORIOLIS_MAX * (2.0 * (first_row + (r + 0.5)) / total_rows - 1.0)

            def around(f):
                mid = ext[step, c, f, r + 1]
                j = f * rows + r
                e = jnp.where(wide == width - 1, from_east[:, j:j + 1], pltpu.roll(mid, width - 1, 1))
                w = jnp.where(wide == 0, from_west[:, j:j + 1], pltpu.roll(mid, 1, 1))
                return mid, e, w, ext[step, c, f, r + 2], ext[step, c, f, r]

            h, he, hw, hn, hs = around(0)
            u, ue, uw, un, us = around(1)
            v, ve, vw, vn, vs = around(2)
            half = 0.5 * COURANT
            h_new = (h - half * (((1.0 + he) * ue - (1.0 + hw) * uw) + ((1.0 + hn) * vn - (1.0 + hs) * vs))
                     + DIFFUSION * (he + hw + hn + hs - 4.0 * h) + FORCE_STEP * pushes[r])
            u_new = (u - half * ((he - hw) + u * (ue - uw) + v * (un - us))
                     + COURANT * coriolis * v + DIFFUSION * (ue + uw + un + us - 4.0 * u))
            v_new = (v - half * ((hn - hs) + u * (ve - vw) + v * (vn - vs))
                     - COURANT * coriolis * u + DIFFUSION * (ve + vw + vn + vs - 4.0 * v))
            put(r, h_new, u_new, v_new)

    @pl.loop(0, chunks)
    def _(c):
        hand_on(0, c)
        receive(0, c)
        load_force(c).wait()

        def put(r, *new):
            for f in range(3):
                ext[1, c, f, r + 1] = new[f]

        advance(0, c, put)
        send(1, c)

    for r in range(rows):
        cell = lax.broadcasted_iota(jnp.int32, (width, sites), 0) + r * width
        onehot[r] = jnp.where(cell == index_ref[0], 1.0, 0.0).astype(jnp.bfloat16)

    def save(i):
        return pltpu.make_async_copy(terms.at[i], terms_hbm.at[i], out_sem.at[i])

    @pl.loop(0, chunks)
    def _(c):
        hand_on(1, c)
        receive(1, c)

        def put(r, *new):
            for f in range(3):
                fore[c, f, r] = new[f]

        advance(1, c, put)
        seen = jnp.zeros((CHUNK, sites), jnp.float32)
        for r in range(rows):
            picked = jnp.dot(jnp.concatenate(parts_of(fore[c, 0, r], 3), axis=0), onehot[r],
                             preferred_element_type=jnp.float32)
            seen += (picked[:CHUNK] + picked[CHUNK:2 * CHUNK]) + picked[2 * CHUNK:]
        readings[c] = seen

    seen = readings[...].reshape(members, sites)
    mean = jnp.mean(seen, axis=0, keepdims=True)
    spread = seen - mean
    inv = 1.0 / error_ref[0]
    innovation = inv * (value_ref[0] - mean)
    left = jnp.concatenate([spread * inv, jnp.broadcast_to(innovation, (8, sites))], axis=0)
    acc[0] = fold(product(left, spread.T))
    swaps = [pltpu.make_async_remote_copy(
        src_ref=acc.at[s], dst_ref=acc_in.at[s], send_sem=sum_send.at[s], recv_sem=sum_recv.at[s],
        device_id=dev(place), device_id_type=MESH) for s, place in enumerate(partners)]
    items = 3 * rows
    for s, swap in enumerate(swaps):
        swap.start()

        @pl.loop(s * items // len(swaps), (s + 1) * items // len(swaps))
        def _(i):
            cells = fore[:, i // rows, lax.rem(i, rows)].reshape(members, width)
            mean = jnp.mean(cells, axis=0, keepdims=True)
            terms[i] = jnp.concatenate(parts_of(cells - mean, 2), axis=0)
            mean_ref[i] = mean
            save(i).start()

        swap.wait_recv()
        acc[s + 1] = acc[s] + acc_in[s]
    sums_ref[...] = acc[len(swaps)]
    for swap in swaps:
        swap.wait_send()

    @pl.loop(0, chunks)
    def _(c):
        for step in range(2):
            @pl.when(has_north)
            def _():
                row_copy(step, c, 0).wait_send()

            @pl.when(has_south)
            def _():
                row_copy(step, c, 1).wait_send()

            @pl.when(detoured(c, detours_by))
            def _():
                onward_copy(step, c).wait_send()

            col_copy(step, c, 0).wait_send()
            col_copy(step, c, 1).wait_send()

    @pl.loop(0, items)
    def _(i):
        save(i).wait()


def analysis_kernel(sums_ref, terms_ref, mean_ref, out_ref, mix, moved):
    members = sums_ref.shape[1]
    half = members // 2
    rows = terms_ref.shape[0]

    @pl.when(pl.program_id(0) == 0)
    def _():
        eye = (lax.broadcasted_iota(jnp.int32, (members, members), 0)
               == lax.broadcasted_iota(jnp.int32, (members, members), 1)).astype(jnp.float32)
        amat = (members - 1) * eye + unfold(sums_ref[...])
        scale = jnp.sqrt(jnp.sum(jnp.sum(amat * amat, axis=1, keepdims=True), axis=0, keepdims=True))

        def turn(_, pair):
            upper, lower = pair
            factor = 1.5 * eye - 0.5 * paired(lower, upper)
            both = paired(jnp.concatenate([upper, lower], axis=0), factor)
            return both[:members], both[members:]

        upper = amat / scale
        lower = 1.5 * eye - 0.5 * upper
        upper = paired(upper, lower)
        upper, lower = lax.fori_loop(1, NS_ITERS - 1, turn, (upper, lower))
        lower = paired(lower, 1.5 * eye - 0.5 * paired(lower, upper))
        root = lower / jnp.sqrt(scale)
        inverse = paired(root, root)
        shift = paired(sums_ref[half:], inverse.T)
        weights = math.sqrt(members - 1) * root.T + shift[0:1, :]
        high = weights.astype(jnp.bfloat16)
        low = (weights - high.astype(jnp.float32)).astype(jnp.bfloat16)
        mix[:members, :members] = high
        mix[:members, members:] = high
        mix[members:, :members] = low
        mix[members:, members:] = jnp.zeros_like(low)

    for r in range(rows):
        both = jnp.dot(mix[...], terms_ref[r], preferred_element_type=jnp.float32)
        moved[r] = mean_ref[r] + both[:members] + both[members:]
    for m in range(0, members, CHUNK):
        out_ref[m:m + CHUNK, 0] = jnp.swapaxes(moved[:, m:m + CHUNK], 0, 1)


def shards(n_lat, n_lon, ocean_status, height_driver, obs_index, obs_value, obs_error):
    members, fields, rows, width = ocean_status.shape
    chunks = members // CHUNK
    sites = obs_index.shape[-1]
    vmem = pl.BlockSpec(memory_space=pltpu.VMEM)
    anywhere = pl.BlockSpec(memory_space=pl.ANY)
    stages = len(doublings(n_lon)) + len(doublings(n_lat))
    dma = pltpu.SemaphoreType.DMA
    f32 = jnp.float32
    block = (chunks, fields, rows, CHUNK, width)
    terms, mean, sums = pl.pallas_call(
        functools.partial(forecast_kernel, n_lat, n_lon),
        out_shape=(jax.ShapeDtypeStruct((fields * rows, 2 * members, width), jnp.bfloat16),
                   jax.ShapeDtypeStruct((fields * rows, 1, width), f32),
                   jax.ShapeDtypeStruct((members // 2 + 8, members), f32)),
        in_specs=[anywhere, anywhere, vmem, vmem, vmem],
        out_specs=(anywhere, vmem, vmem),
        scratch_shapes=[
            pltpu.VMEM((chunks, CHUNK, fields, rows, width), f32),
            pltpu.VMEM((chunks, CHUNK, rows, width), height_driver.dtype),
            pltpu.VMEM((2, chunks, fields, rows + 2, CHUNK, width), f32),
            pltpu.VMEM((2, chunks, fields, CHUNK, width), f32),
            pltpu.VMEM((2, 2, chunks, CHUNK, LANES), f32),
            pltpu.VMEM((2, 2, chunks, CHUNK, LANES), f32),
            pltpu.VMEM(block, f32),
            pltpu.VMEM((fields * rows, 2 * members, width), jnp.bfloat16),
            pltpu.VMEM((rows, width, sites), jnp.bfloat16),
            pltpu.VMEM((chunks, CHUNK, sites), f32),
            pltpu.VMEM((stages + 1, members // 2 + 8, members), f32),
            pltpu.VMEM((stages, members // 2 + 8, members), f32),
            dma((chunks,)), dma((chunks,)), dma((fields * rows,)),
            dma((2, 2, chunks)), dma((2, 2, chunks)),
            dma((2, chunks)), dma((2, chunks)),
            dma((2, 2, chunks)), dma((2, 2, chunks)),
            dma((stages,)), dma((stages,)),
        ],
        compiler_params=pltpu.CompilerParams(collective_id=0, has_side_effects=True, vmem_limit_bytes=63 << 20),
        name="forecast",
    )(ocean_status, height_driver, obs_index, obs_value, obs_error)
    return pl.pallas_call(
        analysis_kernel,
        grid=(fields,),
        out_shape=jax.ShapeDtypeStruct(ocean_status.shape, f32),
        in_specs=[pl.BlockSpec((members // 2 + 8, members), lambda i: (0, 0)),
                  pl.BlockSpec((rows, 2 * members, width), lambda i: (i, 0, 0)),
                  pl.BlockSpec((rows, 1, width), lambda i: (i, 0, 0))],
        out_specs=pl.BlockSpec((members, 1, rows, width), lambda i: (0, i, 0, 0)),
        scratch_shapes=[pltpu.VMEM((2 * members, 2 * members), jnp.bfloat16),
                        pltpu.VMEM((rows, members, width), f32)],
        compiler_params=pltpu.CompilerParams(vmem_limit_bytes=63 << 20),
        name="analysis",
    )(sums, terms, mean)


def solution(mesh):
    return jax.shard_map(
        functools.partial(shards, mesh.shape["lat"], mesh.shape["lon"]),
        mesh=mesh,
        in_specs=(
            P(None, None, "lat", "lon"),
            P(None, "lat", "lon"),
            P("lat", "lon", None),
            P("lat", "lon", None),
            P("lat", "lon", None),
        ),
        out_specs=P(None, None, "lat", "lon"),
        check_vma=False,
    )
```

```python
import functools
import math

import jax
import jax.numpy as jnp
from jax import lax
from jax.experimental import pallas as pl
from jax.experimental.pallas import tpu as pltpu
from jax.sharding import PartitionSpec as P

NS_ITERS = 14
COURANT = 0.2
DIFFUSION = 0.1
FORCE_STEP = 0.5
CORIOLIS_MAX = 0.3
CHUNK = 8
LAG = 3
LANES = 128
MESH = pl.DeviceIdType.MESH


def doublings(count):
    return [1 << b for b in range(count.bit_length() - 1)]


def parts_of(x, count):
    parts = []
    for _ in range(count):
        parts.append(x.astype(jnp.bfloat16))
        x = x - parts[-1].astype(jnp.float32)
    return parts


def product(a, b):
    rows, columns = a.shape[0], b.shape[1]
    whole = jnp.dot(jnp.concatenate(parts_of(a, 2), axis=0), jnp.concatenate(parts_of(b, 2), axis=1),
                    preferred_element_type=jnp.float32)
    return (whole[:rows, :columns] + whole[:rows, columns:]) + (whole[rows:, :columns] + whole[rows:, columns:])


def paired(a, b):
    columns = b.shape[1]
    terms = jnp.concatenate(parts_of(b, 2), axis=1)
    whole = jnp.dot(jnp.concatenate(parts_of(a, 2), axis=1), jnp.concatenate([terms, terms], axis=0),
                    preferred_element_type=jnp.float32)
    return whole[:, :columns] + whole[:, columns:]


def fold(sums):
    members = sums.shape[1]
    half = members // 2
    row = lax.broadcasted_iota(jnp.int32, (half, members), 0)
    column = lax.broadcasted_iota(jnp.int32, (half, members), 1)
    corner = pltpu.roll(sums[half:members], half, 1)
    mixed = jnp.where((column < half) & (row > column), corner, sums[:half])
    diagonal = jnp.sum(jnp.where(row == column, corner, 0.0), axis=0, keepdims=True)
    place = lax.broadcasted_iota(jnp.int32, (8, members), 0)
    return jnp.concatenate([mixed, jnp.where(place == 0, sums[members:], diagonal)], axis=0)


def unfold(folded):
    half = folded.shape[0] - 8
    members = 2 * half
    row = lax.broadcasted_iota(jnp.int32, (members, members), 0)
    column = lax.broadcasted_iota(jnp.int32, (members, members), 1)
    upper = jnp.concatenate([folded[:half], jnp.zeros((half, members), jnp.float32)], axis=0)
    lower = pltpu.roll(pltpu.roll(upper, half, 0), half, 1)
    diagonal = pltpu.roll(folded[half:], half, 1)[1:2]
    first = jnp.where((column >= half) | (row <= column), upper, upper.T)
    last = jnp.where(column < half, upper.T,
                     jnp.where(row > column, lower, jnp.where(row < column, lower.T, diagonal)))
    return jnp.where(row < half, first, last)


def forecast_kernel(n_lat, n_lon, state_hbm, force_hbm, index_ref, value_ref, error_ref, terms_hbm, mean_ref, sums_ref,
                    raw, force, ext, relay, cols_out, cols_in, fore, terms, onehot, readings, acc, acc_in,
                    in_sem, force_sem, out_sem, row_send, row_recv, relay_recv, relay_send, col_send, col_recv, sum_send, sum_recv):
    chunks = raw.shape[0]
    members = chunks * CHUNK
    sites = index_ref.shape[-1]
    rows, width = raw.shape[3], raw.shape[4]
    lat, lon = lax.axis_index("lat"), lax.axis_index("lon")
    east = (lat, lax.rem(lon + 1, n_lon))
    west = (lat, lax.rem(lon + n_lon - 1, n_lon))
    has_south, has_north = lat > 0, lat < n_lat - 1
    south, north = (jnp.maximum(lat - 1, 0), lon), (jnp.minimum(lat + 1, n_lat - 1), lon)

    planes = n_lat // 2
    parity = lax.rem(lat, 2)
    plane = lat // 2
    detours_out = chunks * (parity * (planes - 1 - plane) + (1 - parity) * plane) // planes
    detours_by = chunks * ((1 - parity) * (planes - 1 - plane) + parity * plane) // planes

    def detoured(c, count):
        return lax.rem((chunks - 1 - c) * count, chunks) >= chunks - count

    def dev(place):
        return {"lat": place[0], "lon": place[1]}

    partners = [(lat, lon ^ d) for d in doublings(n_lon)] + [(lat ^ d, lon) for d in doublings(n_lat)]
    far = [(lat, lon ^ d) for d in doublings(n_lon)[1:]] + [(lat ^ d, lon) for d in doublings(n_lat)[1:]]

    def load(c):
        return pltpu.make_async_copy(state_hbm.at[pl.ds(c * CHUNK, CHUNK)], raw.at[c], in_sem.at[c])

    def load_force(c):
        return pltpu.make_async_copy(force_hbm.at[pl.ds(c * CHUNK, CHUNK)], force.at[c], force_sem.at[c])

    @pl.loop(0, chunks)
    def _(c):
        load(c).start()
        load_force(c).start()

    barrier = pltpu.get_barrier_semaphore()
    for place in [east, west] + far:
        pl.semaphore_signal(barrier, inc=1, device_id=dev(place), device_id_type=MESH)

    @pl.when(has_south)
    def _():
        pl.semaphore_signal(barrier, inc=1, device_id=dev(south), device_id_type=MESH)

    @pl.when(has_north)
    def _():
        pl.semaphore_signal(barrier, inc=1, device_id=dev(north), device_id_type=MESH)

    @pl.when(lat > 1)
    def _():
        pl.semaphore_signal(barrier, inc=1, device_id=dev((jnp.maximum(lat - 2, 0), lon)), device_id_type=MESH)

    @pl.when(lat < n_lat - 2)
    def _():
        pl.semaphore_signal(barrier, inc=1, device_id=dev((jnp.minimum(lat + 2, n_lat - 1), lon)), device_id_type=MESH)

    for r in range(rows):
        cell = lax.broadcasted_iota(jnp.int32, (width, sites), 0) + r * width
        onehot[r] = jnp.where(cell == index_ref[0], 1.0, 0.0).astype(jnp.bfloat16)

    @pl.when(lat == 0)
    def _():
        for step in range(2):
            @pl.loop(0, chunks)
            def _(c):
                ext[step, c, :, 0] = jnp.zeros((3, CHUNK, width), jnp.float32)

    @pl.when(lat == n_lat - 1)
    def _():
        for step in range(2):
            @pl.loop(0, chunks)
            def _(c):
                ext[step, c, :, rows + 1] = jnp.zeros((3, CHUNK, width), jnp.float32)

    present = [has_south, has_north, lat > 1, lat < n_lat - 2]
    pl.semaphore_wait(barrier, 2 + len(far) + sum(there.astype(jnp.int32) for there in present))

    def row_copy(step, c, side):
        return pltpu.make_async_remote_copy(
            src_ref=ext.at[step, c, :, rows if side == 0 else 1],
            dst_ref=ext.at[step, c, :, 0 if side == 0 else rows + 1],
            send_sem=row_send.at[step, side, c], recv_sem=row_recv.at[step, side, c],
            device_id=dev(north if side == 0 else south), device_id_type=MESH)

    def detour_copy(step, c):
        return pltpu.make_async_remote_copy(
            src_ref=ext.at[step, c, :, 1 + (rows - 1) * parity], dst_ref=relay.at[step, c],
            send_sem=row_send.at[step, 1 - parity, c], recv_sem=relay_recv.at[step, c],
            device_id=dev((lat + 1 - 2 * parity, lon)), device_id_type=MESH)

    def onward_copy(step, c):
        return pltpu.make_async_remote_copy(
            src_ref=relay.at[step, c], dst_ref=ext.at[step, c, :, (rows + 1) * parity],
            send_sem=relay_send.at[step, c], recv_sem=row_recv.at[step, parity, c],
            device_id=dev((jnp.clip(lat + 2 - 4 * parity, 0, n_lat - 1), lon)), device_id_type=MESH)

    def hand_on(step, c):
        @pl.when(detoured(c, detours_by))
        def _():
            detour_copy(step, c).wait_recv()
            onward_copy(step, c).start()

    def col_copy(step, c, side):
        return pltpu.make_async_remote_copy(
            src_ref=cols_out.at[step, side, c], dst_ref=cols_in.at[step, side, c],
            send_sem=col_send.at[step, side, c], recv_sem=col_recv.at[step, side, c],
            device_id=dev(east if side == 0 else west), device_id_type=MESH)

    lane = lax.broadcasted_iota(jnp.int32, (CHUNK, LANES), 1)
    wide = lax.broadcasted_iota(jnp.int32, (CHUNK, width), 1)

    def send(step, c):
        by = detoured(c, detours_out)

        @pl.when(by)
        def _():
            detour_copy(step, c).start()

        @pl.when(has_north & jnp.logical_not(by & (parity == 1)))
        def _():
            row_copy(step, c, 0).start()

        @pl.when(has_south & jnp.logical_not(by & (parity == 0)))
        def _():
            row_copy(step, c, 1).start()

        last = jnp.zeros((CHUNK, LANES), jnp.float32)
        first = last
        for f in range(3):
            for r in range(rows):
                j = f * rows + r
                last = jnp.where(lane == j, ext[step, c, f, r + 1, :, width - 1:width], last)
                first = jnp.where(lane == j, ext[step, c, f, r + 1, :, 0:1], first)
        cols_out[step, 0, c] = last
        cols_out[step, 1, c] = first
        col_copy(step, c, 0).start()
        col_copy(step, c, 1).start()

    def receive(step, c):
        @pl.when(has_south)
        def _():
            row_copy(step, c, 0).wait_recv()

        @pl.when(has_north)
        def _():
            row_copy(step, c, 1).wait_recv()

        col_copy(step, c, 0).wait_recv()
        col_copy(step, c, 1).wait_recv()

    total_rows = float(n_lat * rows)
    first_row = (lat * rows).astype(jnp.float32)

    def advance(step, c, put):
        pushes = jnp.swapaxes(force[c].astype(jnp.float32), 0, 1)
        from_west = cols_in[step, 0, c]
        from_east = cols_in[step, 1, c]
        for r in range(rows):
            coriolis = CORIOLIS_MAX * (2.0 * (first_row + (r + 0.5)) / total_rows - 1.0)

            def around(f):
                mid = ext[step, c, f, r + 1]
                j = f * rows + r
                e = jnp.where(wide == width - 1, from_east[:, j:j + 1], pltpu.roll(mid, width - 1, 1))
                w = jnp.where(wide == 0, from_west[:, j:j + 1], pltpu.roll(mid, 1, 1))
                return mid, e, w, ext[step, c, f, r + 2], ext[step, c, f, r]

            h, he, hw, hn, hs = around(0)
            u, ue, uw, un, us = around(1)
            v, ve, vw, vn, vs = around(2)
            half = 0.5 * COURANT
            h_new = (h - half * (((1.0 + he) * ue - (1.0 + hw) * uw) + ((1.0 + hn) * vn - (1.0 + hs) * vs))
                     + DIFFUSION * (he + hw + hn + hs - 4.0 * h) + FORCE_STEP * pushes[r])
            u_new = (u - half * ((he - hw) + u * (ue - uw) + v * (un - us))
                     + COURANT * coriolis * v + DIFFUSION * (ue + uw + un + us - 4.0 * u))
            v_new = (v - half * ((hn - hs) + u * (ve - vw) + v * (vn - vs))
                     - COURANT * coriolis * u + DIFFUSION * (ve + vw + vn + vs - 4.0 * v))
            put(r, h_new, u_new, v_new)

    def save(i):
        return pltpu.make_async_copy(terms.at[i], terms_hbm.at[i], out_sem.at[i])

    def begin(c):
        load(c).wait()
        for f in range(3):
            ext[0, c, f, pl.ds(1, rows)] = jnp.swapaxes(raw[c, :, f], 0, 1)
        send(0, c)

    def first_step(c):
        hand_on(0, c)
        receive(0, c)
        load_force(c).wait()

        def put(r, *new):
            for f in range(3):
                ext[1, c, f, r + 1] = new[f]

        advance(0, c, put)
        send(1, c)

    def second_step(c):
        hand_on(1, c)
        receive(1, c)

        def put(r, *new):
            for f in range(3):
                fore[c, f, r] = new[f]

        advance(1, c, put)
        seen = jnp.zeros((CHUNK, sites), jnp.float32)
        for r in range(rows):
            terms_here = [part.astype(jnp.float32) for part in parts_of(fore[c, 0, r], 3)]
            picked = jnp.dot(jnp.concatenate(terms_here, axis=0).astype(jnp.bfloat16), onehot[r],
                             preferred_element_type=jnp.float32)
            seen += (picked[:CHUNK] + picked[CHUNK:2 * CHUNK]) + picked[2 * CHUNK:]
        readings[c] = seen

    @pl.loop(0, chunks + 2 * LAG)
    def _(t):
        @pl.when(t < chunks)
        def _():
            begin(t)

        @pl.when((t >= LAG) & (t < chunks + LAG))
        def _():
            first_step(t - LAG)

        @pl.when(t >= 2 * LAG)
        def _():
            second_step(t - 2 * LAG)

    seen = readings[...].reshape(members, sites)
    mean = jnp.mean(seen, axis=0, keepdims=True)
    spread = seen - mean
    inv = 1.0 / error_ref[0]
    innovation = inv * (value_ref[0] - mean)
    left = jnp.concatenate([spread * inv, jnp.broadcast_to(innovation, (8, sites))], axis=0)
    acc[0] = fold(product(left, spread.T))
    swaps = [pltpu.make_async_remote_copy(
        src_ref=acc.at[s], dst_ref=acc_in.at[s], send_sem=sum_send.at[s], recv_sem=sum_recv.at[s],
        device_id=dev(place), device_id_type=MESH) for s, place in enumerate(partners)]
    items = 3 * rows
    for s, swap in enumerate(swaps):
        swap.start()

        @pl.loop(s * items // len(swaps), (s + 1) * items // len(swaps))
        def _(i):
            cells = fore[:, i // rows, lax.rem(i, rows)].reshape(members, width)
            mean = jnp.mean(cells, axis=0, keepdims=True)
            terms[i] = jnp.concatenate(parts_of(cells - mean, 2), axis=0)
            mean_ref[i] = mean
            save(i).start()

        swap.wait_recv()
        acc[s + 1] = acc[s] + acc_in[s]
    sums_ref[...] = acc[len(swaps)]
    for swap in swaps:
        swap.wait_send()

    @pl.loop(0, chunks)
    def _(c):
        for step in range(2):
            @pl.when(has_north)
            def _():
                row_copy(step, c, 0).wait_send()

            @pl.when(has_south)
            def _():
                row_copy(step, c, 1).wait_send()

            @pl.when(detoured(c, detours_by))
            def _():
                onward_copy(step, c).wait_send()

            col_copy(step, c, 0).wait_send()
            col_copy(step, c, 1).wait_send()

    @pl.loop(0, items)
    def _(i):
        save(i).wait()


def analysis_kernel(sums_ref, terms_ref, mean_ref, out_ref, mix, moved):
    members = sums_ref.shape[1]
    half = members // 2
    rows = terms_ref.shape[0]

    @pl.when(pl.program_id(0) == 0)
    def _():
        eye = (lax.broadcasted_iota(jnp.int32, (members, members), 0)
               == lax.broadcasted_iota(jnp.int32, (members, members), 1)).astype(jnp.float32)
        amat = (members - 1) * eye + unfold(sums_ref[...])
        scale = jnp.sqrt(jnp.sum(jnp.sum(amat * amat, axis=1, keepdims=True), axis=0, keepdims=True))

        def turn(_, pair):
            upper, lower = pair
            factor = 1.5 * eye - 0.5 * paired(lower, upper)
            return paired(factor, upper), paired(factor, lower)

        upper = amat / scale
        lower = 1.5 * eye - 0.5 * upper
        upper = paired(lower, upper)
        upper, lower = lax.fori_loop(1, NS_ITERS - 1, turn, (upper, lower), unroll=True)
        lower = paired(1.5 * eye - 0.5 * paired(lower, upper), lower)
        root = lower / jnp.sqrt(scale)
        inverse = paired(root, root)
        shift = paired(sums_ref[half:], inverse.T)
        weights = math.sqrt(members - 1) * root.T + shift[0:1, :]
        high = weights.astype(jnp.bfloat16)
        low = (weights - high.astype(jnp.float32)).astype(jnp.bfloat16)
        mix[:members, :members] = high
        mix[:members, members:] = high
        mix[members:, :members] = low
        mix[members:, members:] = jnp.zeros_like(low)

    for r in range(rows):
        both = jnp.dot(mix[...], terms_ref[r], preferred_element_type=jnp.float32)
        moved[r] = mean_ref[r] + both[:members] + both[members:]
    for m in range(0, members, CHUNK):
        out_ref[m:m + CHUNK, 0] = jnp.swapaxes(moved[:, m:m + CHUNK], 0, 1)


def shards(n_lat, n_lon, ocean_status, height_driver, obs_index, obs_value, obs_error):
    members, fields, rows, width = ocean_status.shape
    chunks = members // CHUNK
    sites = obs_index.shape[-1]
    vmem = pl.BlockSpec(memory_space=pltpu.VMEM)
    anywhere = pl.BlockSpec(memory_space=pl.ANY)
    stages = len(doublings(n_lon)) + len(doublings(n_lat))
    dma = pltpu.SemaphoreType.DMA
    f32 = jnp.float32
    block = (chunks, fields, rows, CHUNK, width)
    terms, mean, sums = pl.pallas_call(
        functools.partial(forecast_kernel, n_lat, n_lon),
        out_shape=(jax.ShapeDtypeStruct((fields * rows, 2 * members, width), jnp.bfloat16),
                   jax.ShapeDtypeStruct((fields * rows, 1, width), f32),
                   jax.ShapeDtypeStruct((members // 2 + 8, members), f32)),
        in_specs=[anywhere, anywhere, vmem, vmem, vmem],
        out_specs=(anywhere, vmem, vmem),
        scratch_shapes=[
            pltpu.VMEM((chunks, CHUNK, fields, rows, width), f32),
            pltpu.VMEM((chunks, CHUNK, rows, width), height_driver.dtype),
            pltpu.VMEM((2, chunks, fields, rows + 2, CHUNK, width), f32),
            pltpu.VMEM((2, chunks, fields, CHUNK, width), f32),
            pltpu.VMEM((2, 2, chunks, CHUNK, LANES), f32),
            pltpu.VMEM((2, 2, chunks, CHUNK, LANES), f32),
            pltpu.VMEM(block, f32),
            pltpu.VMEM((fields * rows, 2 * members, width), jnp.bfloat16),
            pltpu.VMEM((rows, width, sites), jnp.bfloat16),
            pltpu.VMEM((chunks, CHUNK, sites), f32),
            pltpu.VMEM((stages + 1, members // 2 + 8, members), f32),
            pltpu.VMEM((stages, members // 2 + 8, members), f32),
            dma((chunks,)), dma((chunks,)), dma((fields * rows,)),
            dma((2, 2, chunks)), dma((2, 2, chunks)),
            dma((2, chunks)), dma((2, chunks)),
            dma((2, 2, chunks)), dma((2, 2, chunks)),
            dma((stages,)), dma((stages,)),
        ],
        compiler_params=pltpu.CompilerParams(collective_id=0, has_side_effects=True, vmem_limit_bytes=63 << 20),
        name="forecast",
    )(ocean_status, height_driver, obs_index, obs_value, obs_error)
    return pl.pallas_call(
        analysis_kernel,
        grid=(fields,),
        out_shape=jax.ShapeDtypeStruct(ocean_status.shape, f32),
        in_specs=[pl.BlockSpec((members // 2 + 8, members), lambda i: (0, 0)),
                  pl.BlockSpec((rows, 2 * members, width), lambda i: (i, 0, 0)),
                  pl.BlockSpec((rows, 1, width), lambda i: (i, 0, 0))],
        out_specs=pl.BlockSpec((members, 1, rows, width), lambda i: (0, i, 0, 0)),
        scratch_shapes=[pltpu.VMEM((2 * members, 2 * members), jnp.bfloat16),
                        pltpu.VMEM((rows, members, width), f32)],
        compiler_params=pltpu.CompilerParams(vmem_limit_bytes=63 << 20),
        name="analysis",
    )(sums, terms, mean)


def solution(mesh):
    return jax.shard_map(
        functools.partial(shards, mesh.shape["lat"], mesh.shape["lon"]),
        mesh=mesh,
        in_specs=(
            P(None, None, "lat", "lon"),
            P(None, "lat", "lon"),
            P("lat", "lon", None),
            P("lat", "lon", None),
            P("lat", "lon", None),
        ),
        out_specs=P(None, None, "lat", "lon"),
        check_vma=False,
    )
```

```python
import functools
import math

import jax
import jax.numpy as jnp
from jax import lax
from jax.experimental import pallas as pl
from jax.experimental.pallas import tpu as pltpu
from jax.sharding import PartitionSpec as P

NS_ITERS = 14
COURANT = 0.2
DIFFUSION = 0.1
FORCE_STEP = 0.5
CORIOLIS_MAX = 0.3
CHUNK = 16
LANES = 128
MESH = pl.DeviceIdType.MESH


def doublings(count):
    return [1 << b for b in range(count.bit_length() - 1)]


def parts_of(x, count):
    parts = []
    for _ in range(count):
        parts.append(x.astype(jnp.bfloat16))
        x = x - parts[-1].astype(jnp.float32)
    return parts


def product(a, b):
    rows, columns = a.shape[0], b.shape[1]
    whole = jnp.dot(jnp.concatenate(parts_of(a, 2), axis=0), jnp.concatenate(parts_of(b, 2), axis=1),
                    preferred_element_type=jnp.float32)
    return (whole[:rows, :columns] + whole[:rows, columns:]) + (whole[rows:, :columns] + whole[rows:, columns:])


def paired(a, b):
    columns = b.shape[1]
    terms = jnp.concatenate(parts_of(b, 2), axis=1)
    whole = jnp.dot(jnp.concatenate(parts_of(a, 2), axis=1), jnp.concatenate([terms, terms], axis=0),
                    preferred_element_type=jnp.float32)
    return whole[:, :columns] + whole[:, columns:]


def fold(sums):
    members = sums.shape[1]
    half = members // 2
    row = lax.broadcasted_iota(jnp.int32, (half, members), 0)
    column = lax.broadcasted_iota(jnp.int32, (half, members), 1)
    corner = pltpu.roll(sums[half:members], half, 1)
    mixed = jnp.where((column < half) & (row > column), corner, sums[:half])
    diagonal = jnp.sum(jnp.where(row == column, corner, 0.0), axis=0, keepdims=True)
    place = lax.broadcasted_iota(jnp.int32, (8, members), 0)
    return jnp.concatenate([mixed, jnp.where(place == 0, sums[members:], diagonal)], axis=0)


def unfold(folded):
    half = folded.shape[0] - 8
    members = 2 * half
    row = lax.broadcasted_iota(jnp.int32, (members, members), 0)
    column = lax.broadcasted_iota(jnp.int32, (members, members), 1)
    upper = jnp.concatenate([folded[:half], jnp.zeros((half, members), jnp.float32)], axis=0)
    lower = pltpu.roll(pltpu.roll(upper, half, 0), half, 1)
    diagonal = pltpu.roll(folded[half:], half, 1)[1:2]
    first = jnp.where((column >= half) | (row <= column), upper, upper.T)
    last = jnp.where(column < half, upper.T,
                     jnp.where(row > column, lower, jnp.where(row < column, lower.T, diagonal)))
    return jnp.where(row < half, first, last)


def forecast_kernel(n_lat, n_lon, state_hbm, force_hbm, index_ref, value_ref, error_ref, terms_hbm, mean_ref, sums_ref,
                    raw, force, ext, relay, cols_out, cols_in, fore, terms, onehot, acc, acc_in,
                    in_sem, force_sem, out_sem, row_send, row_recv, relay_recv, relay_send, col_send, col_recv, sum_send, sum_recv):
    chunks = raw.shape[0]
    members = chunks * CHUNK
    sites = index_ref.shape[-1]
    rows, width = raw.shape[3], raw.shape[4]
    lat, lon = lax.axis_index("lat"), lax.axis_index("lon")
    east = (lat, lax.rem(lon + 1, n_lon))
    west = (lat, lax.rem(lon + n_lon - 1, n_lon))
    has_south, has_north = lat > 0, lat < n_lat - 1
    south, north = (jnp.maximum(lat - 1, 0), lon), (jnp.minimum(lat + 1, n_lat - 1), lon)

    planes = n_lat // 2
    parity = lax.rem(lat, 2)
    plane = lat // 2
    detours_out = chunks * (parity * (planes - 1 - plane) + (1 - parity) * plane) // planes
    detours_by = chunks * ((1 - parity) * (planes - 1 - plane) + parity * plane) // planes

    def detoured(c, count):
        return lax.rem((chunks - 1 - c) * count, chunks) >= chunks - count

    def dev(place):
        return {"lat": place[0], "lon": place[1]}

    partners = [(lat, lon ^ d) for d in doublings(n_lon)] + [(lat ^ d, lon) for d in doublings(n_lat)]
    far = [(lat, lon ^ d) for d in doublings(n_lon)[1:]] + [(lat ^ d, lon) for d in doublings(n_lat)[1:]]

    def load(c):
        return pltpu.make_async_copy(state_hbm.at[pl.ds(c * CHUNK, CHUNK)], raw.at[c], in_sem.at[c])

    def load_force(c):
        return pltpu.make_async_copy(force_hbm.at[pl.ds(c * CHUNK, CHUNK)], force.at[c], force_sem.at[c])

    @pl.loop(0, chunks)
    def _(c):
        load(c).start()
        load_force(c).start()

    barrier = pltpu.get_barrier_semaphore()
    for place in [east, west] + far:
        pl.semaphore_signal(barrier, inc=1, device_id=dev(place), device_id_type=MESH)

    @pl.when(has_south)
    def _():
        pl.semaphore_signal(barrier, inc=1, device_id=dev(south), device_id_type=MESH)

    @pl.when(has_north)
    def _():
        pl.semaphore_signal(barrier, inc=1, device_id=dev(north), device_id_type=MESH)

    @pl.when(lat > 1)
    def _():
        pl.semaphore_signal(barrier, inc=1, device_id=dev((jnp.maximum(lat - 2, 0), lon)), device_id_type=MESH)

    @pl.when(lat < n_lat - 2)
    def _():
        pl.semaphore_signal(barrier, inc=1, device_id=dev((jnp.minimum(lat + 2, n_lat - 1), lon)), device_id_type=MESH)

    for r in range(rows):
        cell = lax.broadcasted_iota(jnp.int32, (width, sites), 0) + r * width
        onehot[r] = jnp.where(cell == index_ref[0], 1.0, 0.0).astype(jnp.bfloat16)

    @pl.when(lat == 0)
    def _():
        for step in range(2):
            @pl.loop(0, chunks)
            def _(c):
                ext[step, c, :, 0] = jnp.zeros((3, CHUNK, width), jnp.float32)

    @pl.when(lat == n_lat - 1)
    def _():
        for step in range(2):
            @pl.loop(0, chunks)
            def _(c):
                ext[step, c, :, rows + 1] = jnp.zeros((3, CHUNK, width), jnp.float32)

    present = [has_south, has_north, lat > 1, lat < n_lat - 2]
    pl.semaphore_wait(barrier, 2 + len(far) + sum(there.astype(jnp.int32) for there in present))

    def row_copy(step, c, side):
        return pltpu.make_async_remote_copy(
            src_ref=ext.at[step, c, :, rows if side == 0 else 1],
            dst_ref=ext.at[step, c, :, 0 if side == 0 else rows + 1],
            send_sem=row_send.at[step, side, c], recv_sem=row_recv.at[step, side, c],
            device_id=dev(north if side == 0 else south), device_id_type=MESH)

    def detour_copy(step, c):
        return pltpu.make_async_remote_copy(
            src_ref=ext.at[step, c, :, 1 + (rows - 1) * parity], dst_ref=relay.at[step, c],
            send_sem=row_send.at[step, 1 - parity, c], recv_sem=relay_recv.at[step, c],
            device_id=dev((lat + 1 - 2 * parity, lon)), device_id_type=MESH)

    def onward_copy(step, c):
        return pltpu.make_async_remote_copy(
            src_ref=relay.at[step, c], dst_ref=ext.at[step, c, :, (rows + 1) * parity],
            send_sem=relay_send.at[step, c], recv_sem=row_recv.at[step, parity, c],
            device_id=dev((jnp.clip(lat + 2 - 4 * parity, 0, n_lat - 1), lon)), device_id_type=MESH)

    def hand_on(step, c):
        @pl.when(detoured(c, detours_by))
        def _():
            detour_copy(step, c).wait_recv()
            onward_copy(step, c).start()

    def col_copy(step, c, side):
        return pltpu.make_async_remote_copy(
            src_ref=cols_out.at[step, side, c], dst_ref=cols_in.at[step, side, c],
            send_sem=col_send.at[step, side, c], recv_sem=col_recv.at[step, side, c],
            device_id=dev(east if side == 0 else west), device_id_type=MESH)

    lane = lax.broadcasted_iota(jnp.int32, (CHUNK, LANES), 1)
    wide = lax.broadcasted_iota(jnp.int32, (CHUNK, width), 1)

    def send_rows(step, c):
        by = detoured(c, detours_out)

        @pl.when(by)
        def _():
            detour_copy(step, c).start()

        @pl.when(has_north & jnp.logical_not(by & (parity == 1)))
        def _():
            row_copy(step, c, 0).start()

        @pl.when(has_south & jnp.logical_not(by & (parity == 0)))
        def _():
            row_copy(step, c, 1).start()

    def send_columns(step, c):
        last = jnp.zeros((CHUNK, LANES), jnp.float32)
        first = last
        for f in range(3):
            for r in range(rows):
                j = f * rows + r
                last = jnp.where(lane == j, ext[step, c, f, r + 1, :, width - 1:width], last)
                first = jnp.where(lane == j, ext[step, c, f, r + 1, :, 0:1], first)
        cols_out[step, 0, c] = last
        cols_out[step, 1, c] = first
        col_copy(step, c, 0).start()
        col_copy(step, c, 1).start()

    def receive(step, c):
        @pl.when(has_south)
        def _():
            row_copy(step, c, 0).wait_recv()

        @pl.when(has_north)
        def _():
            row_copy(step, c, 1).wait_recv()

        col_copy(step, c, 0).wait_recv()
        col_copy(step, c, 1).wait_recv()

    total_rows = float(n_lat * rows)
    first_row = (lat * rows).astype(jnp.float32)

    def advance(step, c, put):
        pushes = jnp.swapaxes(force[c].astype(jnp.float32), 0, 1)
        from_west = cols_in[step, 0, c]
        from_east = cols_in[step, 1, c]
        for r in [0, rows - 1] + list(range(1, rows - 1)):
            coriolis = CORIOLIS_MAX * (2.0 * (first_row + (r + 0.5)) / total_rows - 1.0)

            def around(f):
                mid = ext[step, c, f, r + 1]
                j = f * rows + r
                e = jnp.where(wide == width - 1, from_east[:, j:j + 1], pltpu.roll(mid, width - 1, 1))
                w = jnp.where(wide == 0, from_west[:, j:j + 1], pltpu.roll(mid, 1, 1))
                return mid, e, w, ext[step, c, f, r + 2], ext[step, c, f, r]

            h, he, hw, hn, hs = around(0)
            u, ue, uw, un, us = around(1)
            v, ve, vw, vn, vs = around(2)
            half = 0.5 * COURANT
            h_new = (h - half * (((1.0 + he) * ue - (1.0 + hw) * uw) + ((1.0 + hn) * vn - (1.0 + hs) * vs))
                     + DIFFUSION * (he + hw + hn + hs - 4.0 * h) + FORCE_STEP * pushes[r])
            u_new = (u - half * ((he - hw) + u * (ue - uw) + v * (un - us))
                     + COURANT * coriolis * v + DIFFUSION * (ue + uw + un + us - 4.0 * u))
            v_new = (v - half * ((hn - hs) + u * (ve - vw) + v * (vn - vs))
                     - COURANT * coriolis * u + DIFFUSION * (ve + vw + vn + vs - 4.0 * v))
            put(r, h_new, u_new, v_new)

    def save(i):
        return pltpu.make_async_copy(terms.at[i], terms_hbm.at[i], out_sem.at[i])

    def begin(c):
        load(c).wait()
        for f in range(3):
            ext[0, c, f, pl.ds(1, rows)] = jnp.swapaxes(raw[c, :, f], 0, 1)
        send_rows(0, c)
        send_columns(0, c)

    def first_step(c):
        hand_on(0, c)
        receive(0, c)
        load_force(c).wait()

        def put(r, *new):
            for f in range(3):
                ext[1, c, f, r + 1] = new[f]
            if r == rows - 1:
                send_rows(1, c)

        advance(0, c, put)
        send_columns(1, c)

    def second_step(c):
        hand_on(1, c)
        receive(1, c)

        def put(r, *new):
            for f in range(3):
                fore[c, f, r] = new[f]

        advance(1, c, put)

    pl.loop(0, chunks)(begin)
    pl.loop(0, chunks)(first_step)
    pl.loop(0, chunks)(second_step)

    seen = jnp.zeros((members, sites), jnp.float32)
    for r in range(rows):
        terms_here = parts_of(fore[:, 0, r].reshape(members, width), 3)
        picked = jnp.dot(jnp.concatenate(terms_here, axis=0), onehot[r], preferred_element_type=jnp.float32)
        seen += (picked[:members] + picked[members:2 * members]) + picked[2 * members:]
    mean = jnp.mean(seen, axis=0, keepdims=True)
    spread = seen - mean
    inv = 1.0 / error_ref[0]
    innovation = inv * (value_ref[0] - mean)
    left = jnp.concatenate([spread * inv, jnp.broadcast_to(innovation, (8, sites))], axis=0)
    acc[0] = fold(product(left, spread.T))
    swaps = [pltpu.make_async_remote_copy(
        src_ref=acc.at[s], dst_ref=acc_in.at[s], send_sem=sum_send.at[s], recv_sem=sum_recv.at[s],
        device_id=dev(place), device_id_type=MESH) for s, place in enumerate(partners)]
    items = 3 * rows
    for s, swap in enumerate(swaps):
        swap.start()

        @pl.loop(s * items // len(swaps), (s + 1) * items // len(swaps))
        def _(i):
            cells = fore[:, i // rows, lax.rem(i, rows)].reshape(members, width)
            mean = jnp.mean(cells, axis=0, keepdims=True)
            terms[i] = jnp.concatenate(parts_of(cells - mean, 2), axis=0)
            mean_ref[i] = mean
            save(i).start()

        swap.wait_recv()
        acc[s + 1] = acc[s] + acc_in[s]
    sums_ref[...] = acc[len(swaps)]
    for swap in swaps:
        swap.wait_send()

    @pl.loop(0, chunks)
    def _(c):
        for step in range(2):
            @pl.when(has_north)
            def _():
                row_copy(step, c, 0).wait_send()

            @pl.when(has_south)
            def _():
                row_copy(step, c, 1).wait_send()

            @pl.when(detoured(c, detours_by))
            def _():
                onward_copy(step, c).wait_send()

            col_copy(step, c, 0).wait_send()
            col_copy(step, c, 1).wait_send()

    @pl.loop(0, items)
    def _(i):
        save(i).wait()


def analysis_kernel(sums_ref, terms_ref, mean_ref, out_ref, mix, moved):
    members = sums_ref.shape[1]
    half = members // 2
    rows = terms_ref.shape[0]

    @pl.when(pl.program_id(0) == 0)
    def _():
        eye = (lax.broadcasted_iota(jnp.int32, (members, members), 0)
               == lax.broadcasted_iota(jnp.int32, (members, members), 1)).astype(jnp.float32)
        amat = (members - 1) * eye + unfold(sums_ref[...])
        scale = jnp.sqrt(jnp.sum(jnp.sum(amat * amat, axis=1, keepdims=True), axis=0, keepdims=True))

        def turn(_, pair):
            upper, lower = pair
            factor = 1.5 * eye - 0.5 * paired(lower, upper)
            return paired(factor, upper), paired(factor, lower)

        upper = amat / scale
        lower = 1.5 * eye - 0.5 * upper
        upper = paired(lower, upper)
        upper, lower = lax.fori_loop(1, NS_ITERS - 1, turn, (upper, lower), unroll=True)
        lower = paired(1.5 * eye - 0.5 * paired(lower, upper), lower)
        root = lower / jnp.sqrt(scale)
        inverse = paired(root, root)
        shift = paired(sums_ref[half:], inverse.T)
        weights = math.sqrt(members - 1) * root.T + shift[0:1, :]
        high = weights.astype(jnp.bfloat16)
        low = (weights - high.astype(jnp.float32)).astype(jnp.bfloat16)
        mix[:members, :members] = high
        mix[:members, members:] = high
        mix[members:, :members] = low
        mix[members:, members:] = jnp.zeros_like(low)

    for r in range(rows):
        both = jnp.dot(mix[...], terms_ref[r], preferred_element_type=jnp.float32)
        moved[r] = mean_ref[r] + both[:members] + both[members:]
    for m in range(0, members, CHUNK):
        out_ref[m:m + CHUNK, 0] = jnp.swapaxes(moved[:, m:m + CHUNK], 0, 1)


def shards(n_lat, n_lon, ocean_status, height_driver, obs_index, obs_value, obs_error):
    members, fields, rows, width = ocean_status.shape
    chunks = members // CHUNK
    sites = obs_index.shape[-1]
    vmem = pl.BlockSpec(memory_space=pltpu.VMEM)
    anywhere = pl.BlockSpec(memory_space=pl.ANY)
    stages = len(doublings(n_lon)) + len(doublings(n_lat))
    dma = pltpu.SemaphoreType.DMA
    f32 = jnp.float32
    block = (chunks, fields, rows, CHUNK, width)
    terms, mean, sums = pl.pallas_call(
        functools.partial(forecast_kernel, n_lat, n_lon),
        out_shape=(jax.ShapeDtypeStruct((fields * rows, 2 * members, width), jnp.bfloat16),
                   jax.ShapeDtypeStruct((fields * rows, 1, width), f32),
                   jax.ShapeDtypeStruct((members // 2 + 8, members), f32)),
        in_specs=[anywhere, anywhere, vmem, vmem, vmem],
        out_specs=(anywhere, vmem, vmem),
        scratch_shapes=[
            pltpu.VMEM((chunks, CHUNK, fields, rows, width), f32),
            pltpu.VMEM((chunks, CHUNK, rows, width), height_driver.dtype),
            pltpu.VMEM((2, chunks, fields, rows + 2, CHUNK, width), f32),
            pltpu.VMEM((2, chunks, fields, CHUNK, width), f32),
            pltpu.VMEM((2, 2, chunks, CHUNK, LANES), f32),
            pltpu.VMEM((2, 2, chunks, CHUNK, LANES), f32),
            pltpu.VMEM(block, f32),
            pltpu.VMEM((fields * rows, 2 * members, width), jnp.bfloat16),
            pltpu.VMEM((rows, width, sites), jnp.bfloat16),
            pltpu.VMEM((stages + 1, members // 2 + 8, members), f32),
            pltpu.VMEM((stages, members // 2 + 8, members), f32),
            dma((chunks,)), dma((chunks,)), dma((fields * rows,)),
            dma((2, 2, chunks)), dma((2, 2, chunks)),
            dma((2, chunks)), dma((2, chunks)),
            dma((2, 2, chunks)), dma((2, 2, chunks)),
            dma((stages,)), dma((stages,)),
        ],
        compiler_params=pltpu.CompilerParams(collective_id=0, has_side_effects=True, vmem_limit_bytes=63 << 20),
        name="forecast",
    )(ocean_status, height_driver, obs_index, obs_value, obs_error)
    return pl.pallas_call(
        analysis_kernel,
        grid=(fields,),
        out_shape=jax.ShapeDtypeStruct(ocean_status.shape, f32),
        in_specs=[pl.BlockSpec((members // 2 + 8, members), lambda i: (0, 0)),
                  pl.BlockSpec((rows, 2 * members, width), lambda i: (i, 0, 0)),
                  pl.BlockSpec((rows, 1, width), lambda i: (i, 0, 0))],
        out_specs=pl.BlockSpec((members, 1, rows, width), lambda i: (0, i, 0, 0)),
        scratch_shapes=[pltpu.VMEM((2 * members, 2 * members), jnp.bfloat16),
                        pltpu.VMEM((rows, members, width), f32)],
        compiler_params=pltpu.CompilerParams(vmem_limit_bytes=63 << 20),
        name="analysis",
    )(sums, terms, mean)


def solution(mesh):
    return jax.shard_map(
        functools.partial(shards, mesh.shape["lat"], mesh.shape["lon"]),
        mesh=mesh,
        in_specs=(
            P(None, None, "lat", "lon"),
            P(None, "lat", "lon"),
            P("lat", "lon", None),
            P("lat", "lon", None),
            P("lat", "lon", None),
        ),
        out_specs=P(None, None, "lat", "lon"),
        check_vma=False,
    )
```

```python
import functools
import math

import jax
import jax.numpy as jnp
from jax import lax
from jax.experimental import pallas as pl
from jax.experimental.pallas import tpu as pltpu
from jax.sharding import PartitionSpec as P

NS_ITERS = 14
COURANT = 0.2
DIFFUSION = 0.1
FORCE_STEP = 0.5
CORIOLIS_MAX = 0.3
CHUNK = 16
LANES = 128
MESH = pl.DeviceIdType.MESH


def doublings(count):
    return [1 << b for b in range(count.bit_length() - 1)]


def parts_of(x, count):
    parts = []
    for _ in range(count):
        parts.append(x.astype(jnp.bfloat16))
        x = x - parts[-1].astype(jnp.float32)
    return parts


def product(a, b):
    rows, columns = a.shape[0], b.shape[1]
    whole = jnp.dot(jnp.concatenate(parts_of(a, 2), axis=0), jnp.concatenate(parts_of(b, 2), axis=1),
                    preferred_element_type=jnp.float32)
    return (whole[:rows, :columns] + whole[:rows, columns:]) + (whole[rows:, :columns] + whole[rows:, columns:])


def paired(a, b):
    columns = b.shape[1]
    terms = jnp.concatenate(parts_of(b, 2), axis=1)
    whole = jnp.dot(jnp.concatenate(parts_of(a, 2), axis=1), jnp.concatenate([terms, terms], axis=0),
                    preferred_element_type=jnp.float32)
    return whole[:, :columns] + whole[:, columns:]


def fold(sums):
    members = sums.shape[1]
    half = members // 2
    row = lax.broadcasted_iota(jnp.int32, (half, members), 0)
    column = lax.broadcasted_iota(jnp.int32, (half, members), 1)
    corner = pltpu.roll(sums[half:members], half, 1)
    mixed = jnp.where((column < half) & (row > column), corner, sums[:half])
    diagonal = jnp.sum(jnp.where(row == column, corner, 0.0), axis=0, keepdims=True)
    place = lax.broadcasted_iota(jnp.int32, (8, members), 0)
    return jnp.concatenate([mixed, jnp.where(place == 0, sums[members:], diagonal)], axis=0)


def unfold(folded):
    half = folded.shape[0] - 8
    members = 2 * half
    row = lax.broadcasted_iota(jnp.int32, (members, members), 0)
    column = lax.broadcasted_iota(jnp.int32, (members, members), 1)
    upper = jnp.concatenate([folded[:half], jnp.zeros((half, members), jnp.float32)], axis=0)
    lower = pltpu.roll(pltpu.roll(upper, half, 0), half, 1)
    diagonal = pltpu.roll(folded[half:], half, 1)[1:2]
    first = jnp.where((column >= half) | (row <= column), upper, upper.T)
    last = jnp.where(column < half, upper.T,
                     jnp.where(row > column, lower, jnp.where(row < column, lower.T, diagonal)))
    return jnp.where(row < half, first, last)


def forecast_kernel(n_lat, n_lon, state_hbm, force_hbm, index_ref, value_ref, error_ref, terms_hbm, mean_ref, sums_ref,
                    raw, force, ext, relay, cols_out, cols_in, fore, terms, onehot, readings, acc, acc_in, part, part_in, whole,
                    in_sem, force_sem, out_sem, row_send, row_recv, relay_recv, relay_send, col_send, col_recv, sum_send, sum_recv, cut_send, cut_recv, join_send, join_recv):
    chunks = raw.shape[0]
    members = chunks * CHUNK
    sites = index_ref.shape[-1]
    rows, width = raw.shape[3], raw.shape[4]
    lat, lon = lax.axis_index("lat"), lax.axis_index("lon")
    east = (lat, lax.rem(lon + 1, n_lon))
    west = (lat, lax.rem(lon + n_lon - 1, n_lon))
    has_south, has_north = lat > 0, lat < n_lat - 1
    south, north = (jnp.maximum(lat - 1, 0), lon), (jnp.minimum(lat + 1, n_lat - 1), lon)

    planes = n_lat // 2
    parity = lax.rem(lat, 2)
    plane = lat // 2
    detours_out = chunks * (parity * (planes - 1 - plane) + (1 - parity) * plane) // planes
    detours_by = chunks * ((1 - parity) * (planes - 1 - plane) + parity * plane) // planes

    def detoured(c, count):
        return lax.rem((chunks - 1 - c) * count, chunks) >= chunks - count

    def dev(place):
        return {"lat": place[0], "lon": place[1]}

    far = ([(lat, lax.rem(lon + d, n_lon)) for d in range(1, n_lon)]
           + [(lat ^ d, lon) for d in doublings(n_lat)[1:]])

    def load(c):
        return pltpu.make_async_copy(state_hbm.at[pl.ds(c * CHUNK, CHUNK)], raw.at[c], in_sem.at[c])

    def load_force(c):
        return pltpu.make_async_copy(force_hbm.at[pl.ds(c * CHUNK, CHUNK)], force.at[c], force_sem.at[c])

    @pl.loop(0, chunks)
    def _(c):
        load(c).start()
        load_force(c).start()

    barrier = pltpu.get_barrier_semaphore()
    for place in far:
        pl.semaphore_signal(barrier, inc=1, device_id=dev(place), device_id_type=MESH)

    @pl.when(has_south)
    def _():
        pl.semaphore_signal(barrier, inc=1, device_id=dev(south), device_id_type=MESH)

    @pl.when(has_north)
    def _():
        pl.semaphore_signal(barrier, inc=1, device_id=dev(north), device_id_type=MESH)

    @pl.when(lat > 1)
    def _():
        pl.semaphore_signal(barrier, inc=1, device_id=dev((jnp.maximum(lat - 2, 0), lon)), device_id_type=MESH)

    @pl.when(lat < n_lat - 2)
    def _():
        pl.semaphore_signal(barrier, inc=1, device_id=dev((jnp.minimum(lat + 2, n_lat - 1), lon)), device_id_type=MESH)

    for r in range(rows):
        cell = lax.broadcasted_iota(jnp.int32, (width, sites), 0) + r * width
        onehot[r] = jnp.where(cell == index_ref[0], 1.0, 0.0).astype(jnp.bfloat16)

    @pl.when(lat == 0)
    def _():
        for step in range(2):
            @pl.loop(0, chunks)
            def _(c):
                ext[step, c, :, 0] = jnp.zeros((3, CHUNK, width), jnp.float32)

    @pl.when(lat == n_lat - 1)
    def _():
        for step in range(2):
            @pl.loop(0, chunks)
            def _(c):
                ext[step, c, :, rows + 1] = jnp.zeros((3, CHUNK, width), jnp.float32)

    present = [has_south, has_north, lat > 1, lat < n_lat - 2]
    pl.semaphore_wait(barrier, len(far) + sum(there.astype(jnp.int32) for there in present))

    def row_copy(step, c, side):
        return pltpu.make_async_remote_copy(
            src_ref=ext.at[step, c, :, rows if side == 0 else 1],
            dst_ref=ext.at[step, c, :, 0 if side == 0 else rows + 1],
            send_sem=row_send.at[step, side, c], recv_sem=row_recv.at[step, side, c],
            device_id=dev(north if side == 0 else south), device_id_type=MESH)

    def detour_copy(step, c):
        return pltpu.make_async_remote_copy(
            src_ref=ext.at[step, c, :, 1 + (rows - 1) * parity], dst_ref=relay.at[step, c],
            send_sem=row_send.at[step, 1 - parity, c], recv_sem=relay_recv.at[step, c],
            device_id=dev((lat + 1 - 2 * parity, lon)), device_id_type=MESH)

    def onward_copy(step, c):
        return pltpu.make_async_remote_copy(
            src_ref=relay.at[step, c], dst_ref=ext.at[step, c, :, (rows + 1) * parity],
            send_sem=relay_send.at[step, c], recv_sem=row_recv.at[step, parity, c],
            device_id=dev((jnp.clip(lat + 2 - 4 * parity, 0, n_lat - 1), lon)), device_id_type=MESH)

    def hand_on(step, c):
        @pl.when(detoured(c, detours_by))
        def _():
            detour_copy(step, c).wait_recv()
            onward_copy(step, c).start()

    def col_copy(step, c, side):
        return pltpu.make_async_remote_copy(
            src_ref=cols_out.at[step, side, c], dst_ref=cols_in.at[step, side, c],
            send_sem=col_send.at[step, side, c], recv_sem=col_recv.at[step, side, c],
            device_id=dev(east if side == 0 else west), device_id_type=MESH)

    lane = lax.broadcasted_iota(jnp.int32, (CHUNK, LANES), 1)
    wide = lax.broadcasted_iota(jnp.int32, (CHUNK, width), 1)

    def send_rows(step, c):
        by = detoured(c, detours_out)

        @pl.when(by)
        def _():
            detour_copy(step, c).start()

        @pl.when(has_north & jnp.logical_not(by & (parity == 1)))
        def _():
            row_copy(step, c, 0).start()

        @pl.when(has_south & jnp.logical_not(by & (parity == 0)))
        def _():
            row_copy(step, c, 1).start()

    def send_columns(step, c):
        last = jnp.zeros((CHUNK, LANES), jnp.float32)
        first = last
        for f in range(3):
            for r in range(rows):
                j = f * rows + r
                last = jnp.where(lane == j, ext[step, c, f, r + 1, :, width - 1:width], last)
                first = jnp.where(lane == j, ext[step, c, f, r + 1, :, 0:1], first)
        cols_out[step, 0, c] = last
        cols_out[step, 1, c] = first
        col_copy(step, c, 0).start()
        col_copy(step, c, 1).start()

    def receive(step, c):
        @pl.when(has_south)
        def _():
            row_copy(step, c, 0).wait_recv()

        @pl.when(has_north)
        def _():
            row_copy(step, c, 1).wait_recv()

        col_copy(step, c, 0).wait_recv()
        col_copy(step, c, 1).wait_recv()

    total_rows = float(n_lat * rows)
    first_row = (lat * rows).astype(jnp.float32)

    def advance(step, c, put):
        pushes = jnp.swapaxes(force[c].astype(jnp.float32), 0, 1)
        from_west = cols_in[step, 0, c]
        from_east = cols_in[step, 1, c]
        for r in [0, rows - 1] + list(range(1, rows - 1)):
            coriolis = CORIOLIS_MAX * (2.0 * (first_row + (r + 0.5)) / total_rows - 1.0)

            def around(f):
                mid = ext[step, c, f, r + 1]
                j = f * rows + r
                e = jnp.where(wide == width - 1, from_east[:, j:j + 1], pltpu.roll(mid, width - 1, 1))
                w = jnp.where(wide == 0, from_west[:, j:j + 1], pltpu.roll(mid, 1, 1))
                return mid, e, w, ext[step, c, f, r + 2], ext[step, c, f, r]

            h, he, hw, hn, hs = around(0)
            u, ue, uw, un, us = around(1)
            v, ve, vw, vn, vs = around(2)
            half = 0.5 * COURANT
            h_new = (h - half * (((1.0 + he) * ue - (1.0 + hw) * uw) + ((1.0 + hn) * vn - (1.0 + hs) * vs))
                     + DIFFUSION * (he + hw + hn + hs - 4.0 * h) + FORCE_STEP * pushes[r])
            u_new = (u - half * ((he - hw) + u * (ue - uw) + v * (un - us))
                     + COURANT * coriolis * v + DIFFUSION * (ue + uw + un + us - 4.0 * u))
            v_new = (v - half * ((hn - hs) + u * (ve - vw) + v * (vn - vs))
                     - COURANT * coriolis * u + DIFFUSION * (ve + vw + vn + vs - 4.0 * v))
            put(r, h_new, u_new, v_new)

    def save(i):
        return pltpu.make_async_copy(terms.at[i], terms_hbm.at[i], out_sem.at[i])

    def begin(c):
        load(c).wait()
        for f in range(3):
            ext[0, c, f, pl.ds(1, rows)] = jnp.swapaxes(raw[c, :, f], 0, 1)
        send_rows(0, c)
        send_columns(0, c)

    def first_step(c):
        hand_on(0, c)
        receive(0, c)
        load_force(c).wait()

        def put(r, *new):
            for f in range(3):
                ext[1, c, f, r + 1] = new[f]
            if r == rows - 1:
                send_rows(1, c)

        advance(0, c, put)
        send_columns(1, c)

    def second_step(c):
        hand_on(1, c)
        receive(1, c)

        def put(r, *new):
            for f in range(3):
                fore[c, f, r] = new[f]

        advance(1, c, put)
        seen = jnp.zeros((CHUNK, sites), jnp.float32)
        for r in range(rows):
            picked = jnp.dot(jnp.concatenate(parts_of(fore[c, 0, r], 3), axis=0), onehot[r],
                             preferred_element_type=jnp.float32)
            seen += (picked[:CHUNK] + picked[CHUNK:2 * CHUNK]) + picked[2 * CHUNK:]
        readings[c] = seen

    pl.loop(0, chunks)(begin)
    pl.loop(0, chunks)(first_step)
    pl.loop(0, chunks)(second_step)

    seen = readings[...].reshape(members, sites)
    mean = jnp.mean(seen, axis=0, keepdims=True)
    spread = seen - mean
    inv = 1.0 / error_ref[0]
    innovation = inv * (value_ref[0] - mean)
    left = jnp.concatenate([spread * inv, jnp.broadcast_to(innovation, (8, sites))], axis=0)
    folded = fold(product(left, spread.T))
    acc[:folded.shape[0]] = folded
    acc[folded.shape[0]:] = jnp.zeros((acc.shape[0] - folded.shape[0], members), jnp.float32)
    piece = part.shape[1]

    def rows_of(place):
        return pl.ds(pl.multiple_of(place * piece, 8), piece)

    def cut_copy(d):
        place = lax.rem(lon + d, n_lon)
        return pltpu.make_async_remote_copy(
            src_ref=acc.at[rows_of(place)], dst_ref=acc_in.at[d - 1], send_sem=cut_send.at[d - 1],
            recv_sem=cut_recv.at[d - 1], device_id=dev((lat, place)), device_id_type=MESH)

    def join_copy(d):
        return pltpu.make_async_remote_copy(
            src_ref=whole.at[rows_of(lon)], dst_ref=whole.at[rows_of(lon)], send_sem=join_send.at[d - 1],
            recv_sem=join_recv.at[d - 1], device_id=dev((lat, lax.rem(lon + d, n_lon))), device_id_type=MESH)

    swaps = [pltpu.make_async_remote_copy(
        src_ref=part.at[s], dst_ref=part_in.at[s], send_sem=sum_send.at[s], recv_sem=sum_recv.at[s],
        device_id=dev((lat ^ d, lon)), device_id_type=MESH) for s, d in enumerate(doublings(n_lat))]
    others = range(1, n_lon)
    items = 3 * rows
    slots = len(swaps) + 2

    def split_terms(slot):
        @pl.loop(slot * items // slots, (slot + 1) * items // slots)
        def _(i):
            cells = fore[:, i // rows, lax.rem(i, rows)].reshape(members, width)
            mean = jnp.mean(cells, axis=0, keepdims=True)
            terms[i] = jnp.concatenate(parts_of(cells - mean, 2), axis=0)
            mean_ref[i] = mean
            save(i).start()

    for d in others:
        cut_copy(d).start()
    split_terms(0)
    total = acc[rows_of(lon)]
    for d in others:
        cut_copy(d).wait_recv()
        total += acc_in[d - 1]
    part[0] = total
    for s, swap in enumerate(swaps):
        swap.start()
        split_terms(s + 1)
        swap.wait_recv()
        part[s + 1] = part[s] + part_in[s]
    whole[rows_of(lon)] = part[len(swaps)]
    for d in others:
        join_copy(d).start()
    split_terms(slots - 1)
    for d in others:
        join_copy(d).wait_recv()
    sums_ref[...] = whole[:sums_ref.shape[0]]
    for d in others:
        cut_copy(d).wait_send()
        join_copy(d).wait_send()
    for swap in swaps:
        swap.wait_send()

    @pl.loop(0, chunks)
    def _(c):
        for step in range(2):
            @pl.when(has_north)
            def _():
                row_copy(step, c, 0).wait_send()

            @pl.when(has_south)
            def _():
                row_copy(step, c, 1).wait_send()

            @pl.when(detoured(c, detours_by))
            def _():
                onward_copy(step, c).wait_send()

            col_copy(step, c, 0).wait_send()
            col_copy(step, c, 1).wait_send()

    @pl.loop(0, items)
    def _(i):
        save(i).wait()


def analysis_kernel(sums_ref, terms_ref, mean_ref, out_ref, mix, moved):
    members = sums_ref.shape[1]
    half = members // 2
    rows = terms_ref.shape[0]

    @pl.when((pl.program_id(0) == 0) & (pl.program_id(1) == 0))
    def _():
        eye = (lax.broadcasted_iota(jnp.int32, (members, members), 0)
               == lax.broadcasted_iota(jnp.int32, (members, members), 1)).astype(jnp.float32)
        amat = (members - 1) * eye + unfold(sums_ref[...])
        scale = jnp.sqrt(jnp.sum(jnp.sum(amat * amat, axis=1, keepdims=True), axis=0, keepdims=True))

        def turn(_, pair):
            upper, lower = pair
            factor = 1.5 * eye - 0.5 * paired(lower, upper)
            return paired(factor, upper), paired(factor, lower)

        upper = amat / scale
        lower = 1.5 * eye - 0.5 * upper
        upper = paired(lower, upper)
        upper, lower = lax.fori_loop(1, NS_ITERS - 1, turn, (upper, lower), unroll=True)
        lower = paired(1.5 * eye - 0.5 * paired(lower, upper), lower)
        root = lower / jnp.sqrt(scale)
        inverse = paired(root, root)
        shift = paired(sums_ref[half:], inverse.T)
        weights = math.sqrt(members - 1) * root.T + shift[0:1, :]
        high = weights.astype(jnp.bfloat16)
        low = (weights - high.astype(jnp.float32)).astype(jnp.bfloat16)
        mix[:members, :members] = high
        mix[:members, members:] = high
        mix[members:, :members] = low
        mix[members:, members:] = jnp.zeros_like(low)

    for r in range(rows):
        both = jnp.dot(mix[...], terms_ref[r], preferred_element_type=jnp.float32)
        moved[r] = mean_ref[r] + both[:members] + both[members:]
    for m in range(0, members, CHUNK):
        out_ref[m:m + CHUNK, 0] = jnp.swapaxes(moved[:, m:m + CHUNK], 0, 1)


def shards(n_lat, n_lon, ocean_status, height_driver, obs_index, obs_value, obs_error):
    members, fields, rows, width = ocean_status.shape
    chunks = members // CHUNK
    sites = obs_index.shape[-1]
    vmem = pl.BlockSpec(memory_space=pltpu.VMEM)
    anywhere = pl.BlockSpec(memory_space=pl.ANY)
    stages = len(doublings(n_lat))
    piece = 8 * -(-(members // 2 + 8) // (8 * n_lon))
    dma = pltpu.SemaphoreType.DMA
    f32 = jnp.float32
    block = (chunks, fields, rows, CHUNK, width)
    terms, mean, sums = pl.pallas_call(
        functools.partial(forecast_kernel, n_lat, n_lon),
        out_shape=(jax.ShapeDtypeStruct((fields * rows, 2 * members, width), jnp.bfloat16),
                   jax.ShapeDtypeStruct((fields * rows, 1, width), f32),
                   jax.ShapeDtypeStruct((members // 2 + 8, members), f32)),
        in_specs=[anywhere, anywhere, vmem, vmem, vmem],
        out_specs=(anywhere, vmem, vmem),
        scratch_shapes=[
            pltpu.VMEM((chunks, CHUNK, fields, rows, width), f32),
            pltpu.VMEM((chunks, CHUNK, rows, width), height_driver.dtype),
            pltpu.VMEM((2, chunks, fields, rows + 2, CHUNK, width), f32),
            pltpu.VMEM((2, chunks, fields, CHUNK, width), f32),
            pltpu.VMEM((2, 2, chunks, CHUNK, LANES), f32),
            pltpu.VMEM((2, 2, chunks, CHUNK, LANES), f32),
            pltpu.VMEM(block, f32),
            pltpu.VMEM((fields * rows, 2 * members, width), jnp.bfloat16),
            pltpu.VMEM((rows, width, sites), jnp.bfloat16),
            pltpu.VMEM((chunks, CHUNK, sites), f32),
            pltpu.VMEM((piece * n_lon, members), f32),
            pltpu.VMEM((n_lon - 1, piece, members), f32),
            pltpu.VMEM((stages + 1, piece, members), f32),
            pltpu.VMEM((stages, piece, members), f32),
            pltpu.VMEM((piece * n_lon, members), f32),
            dma((chunks,)), dma((chunks,)), dma((fields * rows,)),
            dma((2, 2, chunks)), dma((2, 2, chunks)),
            dma((2, chunks)), dma((2, chunks)),
            dma((2, 2, chunks)), dma((2, 2, chunks)),
            dma((stages,)), dma((stages,)),
            dma((n_lon - 1,)), dma((n_lon - 1,)), dma((n_lon - 1,)), dma((n_lon - 1,)),
        ],
        compiler_params=pltpu.CompilerParams(collective_id=0, has_side_effects=True, vmem_limit_bytes=63 << 20),
        name="forecast",
    )(ocean_status, height_driver, obs_index, obs_value, obs_error)
    return pl.pallas_call(
        analysis_kernel,
        grid=(fields, 2),
        out_shape=jax.ShapeDtypeStruct(ocean_status.shape, f32),
        in_specs=[pl.BlockSpec((members // 2 + 8, members), lambda i, j: (0, 0)),
                  pl.BlockSpec((rows, 2 * members, width // 2), lambda i, j: (i, 0, j)),
                  pl.BlockSpec((rows, 1, width // 2), lambda i, j: (i, 0, j))],
        out_specs=pl.BlockSpec((members, 1, rows, width // 2), lambda i, j: (0, i, 0, j)),
        scratch_shapes=[pltpu.VMEM((2 * members, 2 * members), jnp.bfloat16),
                        pltpu.VMEM((rows, members, width // 2), f32)],
        compiler_params=pltpu.CompilerParams(vmem_limit_bytes=63 << 20),
        name="analysis",
    )(sums, terms, mean)


def solution(mesh):
    return jax.shard_map(
        functools.partial(shards, mesh.shape["lat"], mesh.shape["lon"]),
        mesh=mesh,
        in_specs=(
            P(None, None, "lat", "lon"),
            P(None, "lat", "lon"),
            P("lat", "lon", None),
            P("lat", "lon", None),
            P("lat", "lon", None),
        ),
        out_specs=P(None, None, "lat", "lon"),
        check_vma=False,
    )
```

```python
import functools
import math

import jax
import jax.numpy as jnp
from jax import lax
from jax.experimental import pallas as pl
from jax.experimental.pallas import tpu as pltpu
from jax.sharding import PartitionSpec as P

NS_ITERS = 14
COURANT = 0.2
DIFFUSION = 0.1
FORCE_STEP = 0.5
CORIOLIS_MAX = 0.3
CHUNK = 16
LANES = 128
MESH = pl.DeviceIdType.MESH


def doublings(count):
    return [1 << b for b in range(count.bit_length() - 1)]


def parts_of(x, count):
    parts = []
    for _ in range(count):
        parts.append(x.astype(jnp.bfloat16))
        x = x - parts[-1].astype(jnp.float32)
    return parts


def product(a, b):
    rows, columns = a.shape[0], b.shape[1]
    whole = jnp.dot(jnp.concatenate(parts_of(a, 2), axis=0), jnp.concatenate(parts_of(b, 2), axis=1),
                    preferred_element_type=jnp.float32)
    return (whole[:rows, :columns] + whole[:rows, columns:]) + (whole[rows:, :columns] + whole[rows:, columns:])


def paired(a, b):
    columns = b.shape[1]
    terms = jnp.concatenate(parts_of(b, 2), axis=1)
    whole = jnp.dot(jnp.concatenate(parts_of(a, 2), axis=1), jnp.concatenate([terms, terms], axis=0),
                    preferred_element_type=jnp.float32)
    return whole[:, :columns] + whole[:, columns:]


def fold(sums):
    members = sums.shape[1]
    half = members // 2
    row = lax.broadcasted_iota(jnp.int32, (half, members), 0)
    column = lax.broadcasted_iota(jnp.int32, (half, members), 1)
    corner = pltpu.roll(sums[half:members], half, 1)
    mixed = jnp.where((column < half) & (row > column), corner, sums[:half])
    diagonal = jnp.sum(jnp.where(row == column, corner, 0.0), axis=0, keepdims=True)
    place = lax.broadcasted_iota(jnp.int32, (8, members), 0)
    return jnp.concatenate([mixed, jnp.where(place == 0, sums[members:], diagonal)], axis=0)


def unfold(folded):
    half = folded.shape[0] - 8
    members = 2 * half
    row = lax.broadcasted_iota(jnp.int32, (members, members), 0)
    column = lax.broadcasted_iota(jnp.int32, (members, members), 1)
    upper = jnp.concatenate([folded[:half], jnp.zeros((half, members), jnp.float32)], axis=0)
    lower = pltpu.roll(pltpu.roll(upper, half, 0), half, 1)
    diagonal = pltpu.roll(folded[half:], half, 1)[1:2]
    first = jnp.where((column >= half) | (row <= column), upper, upper.T)
    last = jnp.where(column < half, upper.T,
                     jnp.where(row > column, lower, jnp.where(row < column, lower.T, diagonal)))
    return jnp.where(row < half, first, last)


def forecast_kernel(n_lat, n_lon, state_hbm, force_hbm, index_ref, value_ref, error_ref, terms_hbm, mean_ref, sums_ref,
                    raw, force, ext, relay, cols_out, cols_in, fore, terms, onehot, readings, acc, acc_in,
                    in_sem, force_sem, out_sem, row_send, row_recv, relay_recv, relay_send, col_send, col_recv, sum_send, sum_recv):
    chunks = raw.shape[0]
    members = chunks * CHUNK
    sites = index_ref.shape[-1]
    rows, width = raw.shape[3], raw.shape[4]
    lat, lon = lax.axis_index("lat"), lax.axis_index("lon")
    east = (lat, lax.rem(lon + 1, n_lon))
    west = (lat, lax.rem(lon + n_lon - 1, n_lon))
    has_south, has_north = lat > 0, lat < n_lat - 1
    south, north = (jnp.maximum(lat - 1, 0), lon), (jnp.minimum(lat + 1, n_lat - 1), lon)

    planes = n_lat // 2
    parity = lax.rem(lat, 2)
    plane = lat // 2
    detours_out = chunks * (parity * (planes - 1 - plane) + (1 - parity) * plane) // planes
    detours_by = chunks * ((1 - parity) * (planes - 1 - plane) + parity * plane) // planes

    def detoured(c, count):
        return lax.rem((chunks - 1 - c) * count, chunks) >= chunks - count

    def dev(place):
        return {"lat": place[0], "lon": place[1]}

    partners = [(lat, lon ^ d) for d in doublings(n_lon)] + [(lat ^ d, lon) for d in doublings(n_lat)]
    far = [(lat, lon ^ d) for d in doublings(n_lon)[1:]] + [(lat ^ d, lon) for d in doublings(n_lat)[1:]]

    def load(c):
        return pltpu.make_async_copy(state_hbm.at[pl.ds(c * CHUNK, CHUNK)], raw.at[c], in_sem.at[c])

    def load_force(c):
        return pltpu.make_async_copy(force_hbm.at[pl.ds(c * CHUNK, CHUNK)], force.at[c], force_sem.at[c])

    @pl.loop(0, chunks)
    def _(c):
        load(c).start()

    @pl.loop(0, chunks)
    def _(c):
        load_force(c).start()

    barrier = pltpu.get_barrier_semaphore()
    for place in [east, west] + far:
        pl.semaphore_signal(barrier, inc=1, device_id=dev(place), device_id_type=MESH)

    @pl.when(has_south)
    def _():
        pl.semaphore_signal(barrier, inc=1, device_id=dev(south), device_id_type=MESH)

    @pl.when(has_north)
    def _():
        pl.semaphore_signal(barrier, inc=1, device_id=dev(north), device_id_type=MESH)

    @pl.when(lat > 1)
    def _():
        pl.semaphore_signal(barrier, inc=1, device_id=dev((jnp.maximum(lat - 2, 0), lon)), device_id_type=MESH)

    @pl.when(lat < n_lat - 2)
    def _():
        pl.semaphore_signal(barrier, inc=1, device_id=dev((jnp.minimum(lat + 2, n_lat - 1), lon)), device_id_type=MESH)

    present = [has_south, has_north, lat > 1, lat < n_lat - 2]
    pl.semaphore_wait(barrier, 2 + len(far) + sum(there.astype(jnp.int32) for there in present))

    def row_copy(step, c, side):
        return pltpu.make_async_remote_copy(
            src_ref=ext.at[step, c, :, rows if side == 0 else 1],
            dst_ref=ext.at[step, c, :, 0 if side == 0 else rows + 1],
            send_sem=row_send.at[step, side, c], recv_sem=row_recv.at[step, side, c],
            device_id=dev(north if side == 0 else south), device_id_type=MESH)

    def detour_copy(step, c):
        return pltpu.make_async_remote_copy(
            src_ref=ext.at[step, c, :, 1 + (rows - 1) * parity], dst_ref=relay.at[step, c],
            send_sem=row_send.at[step, 1 - parity, c], recv_sem=relay_recv.at[step, c],
            device_id=dev((lat + 1 - 2 * parity, lon)), device_id_type=MESH)

    def onward_copy(step, c):
        return pltpu.make_async_remote_copy(
            src_ref=relay.at[step, c], dst_ref=ext.at[step, c, :, (rows + 1) * parity],
            send_sem=relay_send.at[step, c], recv_sem=row_recv.at[step, parity, c],
            device_id=dev((jnp.clip(lat + 2 - 4 * parity, 0, n_lat - 1), lon)), device_id_type=MESH)

    def hand_on(step, c):
        @pl.when(detoured(c, detours_by))
        def _():
            detour_copy(step, c).wait_recv()
            onward_copy(step, c).start()

    def col_copy(step, c, side):
        return pltpu.make_async_remote_copy(
            src_ref=cols_out.at[step, side, c], dst_ref=cols_in.at[step, side, c],
            send_sem=col_send.at[step, side, c], recv_sem=col_recv.at[step, side, c],
            device_id=dev(east if side == 0 else west), device_id_type=MESH)

    lane = lax.broadcasted_iota(jnp.int32, (CHUNK, LANES), 1)
    wide = lax.broadcasted_iota(jnp.int32, (CHUNK, width), 1)

    def send(step, c):
        by = detoured(c, detours_out)

        @pl.when(by)
        def _():
            detour_copy(step, c).start()

        @pl.when(has_north & jnp.logical_not(by & (parity == 1)))
        def _():
            row_copy(step, c, 0).start()

        @pl.when(has_south & jnp.logical_not(by & (parity == 0)))
        def _():
            row_copy(step, c, 1).start()

        last = jnp.zeros((CHUNK, LANES), jnp.float32)
        first = last
        for f in range(3):
            for r in range(rows):
                j = f * rows + r
                last = jnp.where(lane == j, ext[step, c, f, r + 1, :, width - 1:width], last)
                first = jnp.where(lane == j, ext[step, c, f, r + 1, :, 0:1], first)
        cols_out[step, 0, c] = last
        cols_out[step, 1, c] = first
        col_copy(step, c, 0).start()
        col_copy(step, c, 1).start()

    def receive(step, c):
        @pl.when(has_south)
        def _():
            row_copy(step, c, 0).wait_recv()

        @pl.when(has_north)
        def _():
            row_copy(step, c, 1).wait_recv()

        col_copy(step, c, 0).wait_recv()
        col_copy(step, c, 1).wait_recv()

    @pl.when(lat == 0)
    def _():
        for step in range(2):
            @pl.loop(0, chunks)
            def _(c):
                ext[step, c, :, 0] = jnp.zeros((3, CHUNK, width), jnp.float32)

    @pl.when(lat == n_lat - 1)
    def _():
        for step in range(2):
            @pl.loop(0, chunks)
            def _(c):
                ext[step, c, :, rows + 1] = jnp.zeros((3, CHUNK, width), jnp.float32)

    @pl.loop(0, chunks)
    def _(c):
        load(c).wait()
        for f in range(3):
            ext[0, c, f, pl.ds(1, rows)] = jnp.swapaxes(raw[c, :, f], 0, 1)
        send(0, c)

    total_rows = float(n_lat * rows)
    first_row = (lat * rows).astype(jnp.float32)

    def advance(step, c, put):
        pushes = jnp.swapaxes(force[c].astype(jnp.float32), 0, 1)
        from_west = cols_in[step, 0, c]
        from_east = cols_in[step, 1, c]
        for r in range(rows):
            coriolis = CORIOLIS_MAX * (2.0 * (first_row + (r + 0.5)) / total_rows - 1.0)

            def around(f):
                mid = ext[step, c, f, r + 1]
                j = f * rows + r
                e = jnp.where(wide == width - 1, from_east[:, j:j + 1], pltpu.roll(mid, width - 1, 1))
                w = jnp.where(wide == 0, from_west[:, j:j + 1], pltpu.roll(mid, 1, 1))
                return mid, e, w, ext[step, c, f, r + 2], ext[step, c, f, r]

            h, he, hw, hn, hs = around(0)
            u, ue, uw, un, us = around(1)
            v, ve, vw, vn, vs = around(2)
            half = 0.5 * COURANT
            h_new = (h - half * (((1.0 + he) * ue - (1.0 + hw) * uw) + ((1.0 + hn) * vn - (1.0 + hs) * vs))
                     + DIFFUSION * (he + hw + hn + hs - 4.0 * h) + FORCE_STEP * pushes[r])
            u_new = (u - half * ((he - hw) + u * (ue - uw) + v * (un - us))
                     + COURANT * coriolis * v + DIFFUSION * (ue + uw + un + us - 4.0 * u))
            v_new = (v - half * ((hn - hs) + u * (ve - vw) + v * (vn - vs))
                     - COURANT * coriolis * u + DIFFUSION * (ve + vw + vn + vs - 4.0 * v))
            put(r, h_new, u_new, v_new)

    @pl.loop(0, chunks)
    def _(c):
        hand_on(0, c)
        receive(0, c)
        load_force(c).wait()

        def put(r, *new):
            for f in range(3):
                ext[1, c, f, r + 1] = new[f]

        advance(0, c, put)
        send(1, c)

    for r in range(rows):
        cell = lax.broadcasted_iota(jnp.int32, (width, sites), 0) + r * width
        onehot[r] = jnp.where(cell == index_ref[0], 1.0, 0.0).astype(jnp.bfloat16)

    def save(i):
        return pltpu.make_async_copy(terms.at[i], terms_hbm.at[i], out_sem.at[i])

    @pl.loop(0, chunks)
    def _(c):
        hand_on(1, c)
        receive(1, c)

        def put(r, *new):
            for f in range(3):
                fore[c, f, r] = new[f]

        advance(1, c, put)
        seen = jnp.zeros((CHUNK, sites), jnp.float32)
        for r in range(rows):
            picked = jnp.dot(jnp.concatenate(parts_of(fore[c, 0, r], 3), axis=0), onehot[r],
                             preferred_element_type=jnp.float32)
            seen += (picked[:CHUNK] + picked[CHUNK:2 * CHUNK]) + picked[2 * CHUNK:]
        readings[c] = seen

    seen = readings[...].reshape(members, sites)
    mean = jnp.mean(seen, axis=0, keepdims=True)
    spread = seen - mean
    inv = 1.0 / error_ref[0]
    innovation = inv * (value_ref[0] - mean)
    left = jnp.concatenate([spread * inv, jnp.broadcast_to(innovation, (8, sites))], axis=0)
    acc[0] = fold(product(left, spread.T))
    swaps = [pltpu.make_async_remote_copy(
        src_ref=acc.at[s], dst_ref=acc_in.at[s], send_sem=sum_send.at[s], recv_sem=sum_recv.at[s],
        device_id=dev(place), device_id_type=MESH) for s, place in enumerate(partners)]
    items = 3 * rows
    for s, swap in enumerate(swaps):
        swap.start()

        @pl.loop(s * items // len(swaps), (s + 1) * items // len(swaps))
        def _(i):
            cells = fore[:, i // rows, lax.rem(i, rows)].reshape(members, width)
            mean = jnp.mean(cells, axis=0, keepdims=True)
            terms[i] = jnp.concatenate(parts_of(cells - mean, 2), axis=0)
            mean_ref[i] = mean
            save(i).start()

        swap.wait_recv()
        acc[s + 1] = acc[s] + acc_in[s]
    sums_ref[...] = acc[len(swaps)]
    for swap in swaps:
        swap.wait_send()

    @pl.loop(0, chunks)
    def _(c):
        for step in range(2):
            @pl.when(has_north)
            def _():
                row_copy(step, c, 0).wait_send()

            @pl.when(has_south)
            def _():
                row_copy(step, c, 1).wait_send()

            @pl.when(detoured(c, detours_by))
            def _():
                onward_copy(step, c).wait_send()

            col_copy(step, c, 0).wait_send()
            col_copy(step, c, 1).wait_send()

    @pl.loop(0, items)
    def _(i):
        save(i).wait()


def analysis_kernel(sums_ref, terms_ref, mean_ref, out_ref, mix, moved):
    members = sums_ref.shape[1]
    half = members // 2
    rows = terms_ref.shape[0]

    @pl.when(pl.program_id(0) == 0)
    def _():
        eye = (lax.broadcasted_iota(jnp.int32, (members, members), 0)
               == lax.broadcasted_iota(jnp.int32, (members, members), 1)).astype(jnp.float32)
        amat = (members - 1) * eye + unfold(sums_ref[...])
        scale = jnp.sqrt(jnp.sum(jnp.sum(amat * amat, axis=1, keepdims=True), axis=0, keepdims=True))

        def turn(_, pair):
            upper, lower = pair
            factor = 1.5 * eye - 0.5 * paired(lower, upper)
            return paired(factor, upper), paired(factor, lower)

        upper = amat / scale
        lower = 1.5 * eye - 0.5 * upper
        upper = paired(lower, upper)
        upper, lower = lax.fori_loop(1, NS_ITERS - 1, turn, (upper, lower), unroll=True)
        lower = paired(1.5 * eye - 0.5 * paired(lower, upper), lower)
        root = lower / jnp.sqrt(scale)
        inverse = paired(root, root)
        shift = paired(sums_ref[half:], inverse.T)
        weights = math.sqrt(members - 1) * root.T + shift[0:1, :]
        high = weights.astype(jnp.bfloat16)
        low = (weights - high.astype(jnp.float32)).astype(jnp.bfloat16)
        mix[:members, :members] = high
        mix[:members, members:] = high
        mix[members:, :members] = low
        mix[members:, members:] = jnp.zeros_like(low)

    for r in range(rows):
        both = jnp.dot(mix[...], terms_ref[r], preferred_element_type=jnp.float32)
        moved[r] = mean_ref[r] + both[:members] + both[members:]
    for m in range(0, members, CHUNK):
        out_ref[m:m + CHUNK, 0] = jnp.swapaxes(moved[:, m:m + CHUNK], 0, 1)


def shards(n_lat, n_lon, ocean_status, height_driver, obs_index, obs_value, obs_error):
    members, fields, rows, width = ocean_status.shape
    chunks = members // CHUNK
    sites = obs_index.shape[-1]
    vmem = pl.BlockSpec(memory_space=pltpu.VMEM)
    anywhere = pl.BlockSpec(memory_space=pl.ANY)
    stages = len(doublings(n_lon)) + len(doublings(n_lat))
    dma = pltpu.SemaphoreType.DMA
    f32 = jnp.float32
    block = (chunks, fields, rows, CHUNK, width)
    terms, mean, sums = pl.pallas_call(
        functools.partial(forecast_kernel, n_lat, n_lon),
        out_shape=(jax.ShapeDtypeStruct((fields * rows, 2 * members, width), jnp.bfloat16),
                   jax.ShapeDtypeStruct((fields * rows, 1, width), f32),
                   jax.ShapeDtypeStruct((members // 2 + 8, members), f32)),
        in_specs=[anywhere, anywhere, vmem, vmem, vmem],
        out_specs=(anywhere, vmem, vmem),
        scratch_shapes=[
            pltpu.VMEM((chunks, CHUNK, fields, rows, width), f32),
            pltpu.VMEM((chunks, CHUNK, rows, width), height_driver.dtype),
            pltpu.VMEM((2, chunks, fields, rows + 2, CHUNK, width), f32),
            pltpu.VMEM((2, chunks, fields, CHUNK, width), f32),
            pltpu.VMEM((2, 2, chunks, CHUNK, LANES), f32),
            pltpu.VMEM((2, 2, chunks, CHUNK, LANES), f32),
            pltpu.VMEM(block, f32),
            pltpu.VMEM((fields * rows, 2 * members, width), jnp.bfloat16),
            pltpu.VMEM((rows, width, sites), jnp.bfloat16),
            pltpu.VMEM((chunks, CHUNK, sites), f32),
            pltpu.VMEM((stages + 1, members // 2 + 8, members), f32),
            pltpu.VMEM((stages, members // 2 + 8, members), f32),
            dma((chunks,)), dma((chunks,)), dma((fields * rows,)),
            dma((2, 2, chunks)), dma((2, 2, chunks)),
            dma((2, chunks)), dma((2, chunks)),
            dma((2, 2, chunks)), dma((2, 2, chunks)),
            dma((stages,)), dma((stages,)),
        ],
        compiler_params=pltpu.CompilerParams(collective_id=0, has_side_effects=True, vmem_limit_bytes=63 << 20),
        name="forecast",
    )(ocean_status, height_driver, obs_index, obs_value, obs_error)
    return pl.pallas_call(
        analysis_kernel,
        grid=(fields,),
        out_shape=jax.ShapeDtypeStruct(ocean_status.shape, f32),
        in_specs=[pl.BlockSpec((members // 2 + 8, members), lambda i: (0, 0)),
                  pl.BlockSpec((rows, 2 * members, width), lambda i: (i, 0, 0)),
                  pl.BlockSpec((rows, 1, width), lambda i: (i, 0, 0))],
        out_specs=pl.BlockSpec((members, 1, rows, width), lambda i: (0, i, 0, 0)),
        scratch_shapes=[pltpu.VMEM((2 * members, 2 * members), jnp.bfloat16),
                        pltpu.VMEM((rows, members, width), f32)],
        compiler_params=pltpu.CompilerParams(vmem_limit_bytes=63 << 20),
        name="analysis",
    )(sums, terms, mean)


def solution(mesh):
    return jax.shard_map(
        functools.partial(shards, mesh.shape["lat"], mesh.shape["lon"]),
        mesh=mesh,
        in_specs=(
            P(None, None, "lat", "lon"),
            P(None, "lat", "lon"),
            P("lat", "lon", None),
            P("lat", "lon", None),
            P("lat", "lon", None),
        ),
        out_specs=P(None, None, "lat", "lon"),
        check_vma=False,
    )
```
